512 devices in a mesh: fsdp: 16 (over y_lo, x, core), ctx: 32 (over y_hi, z).
Axes of the slice: x: 4, y: 8 (y_hi: 4, y_lo: 2; y = y_hi * 2 + y_lo), z: 8, core: 2. Of those that a mesh axis runs over, the one named last changes fastest.
Arguments:
- queries: bfloat16 [16, 4096, 1024], P('fsdp', 'ctx'), may hold values from -6 to 6
- keys: bfloat16 [16, 4096, 1024], P('fsdp', 'ctx'), may hold values from -8 to 8
- values: bfloat16 [16, 4096, 1024], P('fsdp', 'ctx'), may hold values from -6 to 6
- out_grad: bfloat16 [16, 4096, 2048], P('fsdp', 'ctx'), may hold values from -6 to 6
- weight: bfloat16 [2048, 1024], P('fsdp'), may hold values from -0.1875 to 0.1875
- neighbours: int32 [16, 32, 4], P('fsdp'), may hold values from -1 to 31, as said below
Outputs:
- outputs: bfloat16 [16, 4096, 2048], P('fsdp', 'ctx')
- query_grad: bfloat16 [16, 4096, 1024], P('fsdp', 'ctx')
- key_grad: bfloat16 [16, 4096, 1024], P('fsdp', 'ctx')
- value_grad: bfloat16 [16, 4096, 1024], P('fsdp', 'ctx')
- weight_grad: float32 [2048, 1024], P('fsdp')
The draws below stay inside these ranges and needn't reach their ends.
Inputs may be any that keep to these rules, and one draw needn't show every extreme that they name: `neighbours`: slot 0 of block j is j itself. Each other live slot names a block b with b // 1 at cycle distance 1 to 2 from j // 1 along 32 // 1 positions (cyclic), distinct live slots of one row lying at distinct distances with sign; live slots come first, then -1 padding; slot 1 is always live.
All inputs are finite; a program needn't handle non-finite values.
Results may differ from the reference program's by a relative error of at most 0.034.
Values may be sent and summed in bfloat16 or wider, within the bound.
A program may use at most 64 MiB of HBM per device.

```python
import math
import jax
import jax.numpy as jnp
from jax import lax

D = 2048
HEADS = 8
HDIM = 128
BS = 128
NB = 4
HOPS = 2
BLK_DEV = 1
TOK_DEV = 128
NBLK = 32
SEQ = 4096
SEQS = 16
HW = 1024


def query_key_pair(base_key):
    query_seed = jax.random.fold_in(base_key, 101)
    key_seed = jax.random.fold_in(base_key, 102)
    full_shape = (SEQS, SEQ, HEADS, HDIM)
    query_rows = jnp.clip(jax.random.normal(query_seed, full_shape, jnp.float32), -6.0, 6.0)
    key_rows = jnp.clip(jax.random.normal(key_seed, full_shape, jnp.float32), -6.0, 6.0)
    return (query_rows.reshape(SEQS, SEQ, HEADS * HDIM), key_rows.reshape(SEQS, SEQ, HEADS * HDIM))


def draw_queries(key, part):
    return query_key_pair(key)[0].astype(jnp.bfloat16)


def draw_keys(key, part):
    return query_key_pair(key)[1].astype(jnp.bfloat16)


def draw_neighbours(key, part):
    cycle_size = NBLK // BLK_DEV
    block_ids = jnp.arange(NBLK, dtype=jnp.int32)
    home_dev = block_ids // BLK_DEV
    offset_table = jnp.concatenate([jnp.arange(-HOPS, 0, dtype=jnp.int32), jnp.arange(1, HOPS + 1, dtype=jnp.int32)])
    rank_scores = jax.random.randint(jax.random.fold_in(key, 201), (SEQS, NBLK, 2 * HOPS), 0, 1 << 20) * (2 * HOPS) + jnp.arange(2 * HOPS, dtype=jnp.int32)
    rank_order = jnp.argsort(rank_scores, axis=-1)
    chosen_offsets = offset_table[rank_order][..., :NB - 1]
    within_dev = jax.random.randint(jax.random.fold_in(key, 202), (SEQS, NBLK, NB - 1), 0, BLK_DEV)
    far_blocks = (home_dev[None, :, None] + chosen_offsets) % cycle_size * BLK_DEV + within_dev
    live_count = jax.random.randint(jax.random.fold_in(key, 203), (SEQS, NBLK, 1), 1, NB)
    live_count = jnp.where(block_ids[None, :, None] == 0, NB - 1, live_count)
    slot_number = jnp.arange(1, NB, dtype=jnp.int32)
    far_blocks = jnp.where(slot_number <= live_count, far_blocks, -1)
    own_blocks = jnp.broadcast_to(block_ids[None, :, None], (SEQS, NBLK, 1))
    return jnp.concatenate([own_blocks, far_blocks], axis=-1).astype(jnp.int32)


def strengthened(entries, stream_key, source, target, shards_of, factor):
    def block_of(axis_at):
        return (jnp.arange(entries.shape[axis_at]) // (entries.shape[axis_at] // shards_of)).reshape((-1,) + (1,) * (entries.ndim - 1 - axis_at))

    first = jax.random.permutation(stream_key, shards_of)[block_of(target)]
    second = (block_of(target) + shards_of // 2) % shards_of
    return jnp.where((block_of(source) == first) | (block_of(source) == second), factor * entries, entries)


def steps_of(rng, dims, split, smallest, top_value):
    def one(dim, blocks):
        steps = jax.random.uniform(jax.random.fold_in(jax.random.fold_in(rng, 6), dim), (blocks,), jnp.float32, smallest / len(split), top_value / len(split))
        return jnp.repeat(jnp.exp(steps), dims[dim] // blocks).reshape((-1,) + (1,) * (len(dims) - dim - 1))

    loudness = one(*split[0])
    for cut in split[1:]:
        loudness = loudness * one(*cut)
    return loudness


def normal_values(own_key, shape, scale, bound, pieces=(), kind=jnp.bfloat16):
    values = jax.random.normal(own_key, shape, jnp.float32) * scale
    if len(pieces) > 0:
        values = steps_of(own_key, shape, pieces, -0.22, 0.18) * values
    return jnp.clip(values, min=-bound, max=bound).astype(kind)


def bell_draw_with(key, dims, width, reach, cuts, heavy, kind=jnp.bfloat16):
    drawn = width * jax.random.normal(key, dims, jnp.float32)
    if cuts:
        drawn = drawn * steps_of(key, dims, cuts, -0.22, 0.18)
    return jnp.clip(strengthened(drawn, jax.random.fold_in(key, 3), *heavy), -reach, reach).astype(kind)


def setup_inputs(seed: int = 0) -> dict:
    arg_keys = jax.random.split(jax.random.key(seed), 7)
    return {
        "queries": draw_queries(jax.random.fold_in(arg_keys[6], 71), 0),
        "keys": draw_keys(jax.random.fold_in(arg_keys[6], 71), 0),
        "values": normal_values(arg_keys[2], (SEQS, SEQ, HW), 1.0, 6.0, ((0, 16), (1, 32))),
        "out_grad": bell_draw_with(arg_keys[3], (SEQS, SEQ, D), 1.0, 6.0, ((0, 16), (1, 32)), (0, 2, 16, 2.0)),
        "weight": normal_values(arg_keys[4], (D, HW), HW ** -0.5, 0.1875, ((0, 16),)),
        "neighbours": draw_neighbours(jax.random.fold_in(arg_keys[6], 71), 0),
    }


def to_half(values_in):
    return lax.optimization_barrier(values_in.astype(jnp.bfloat16)).astype(jnp.float32)

def run_sum(slot_terms, safe_blocks, block_count):
    cycle_size = block_count // BLK_DEV
    window_count = (2 * HOPS + 1) * BLK_DEV
    run_index = (jnp.arange(block_count, dtype=jnp.int32) // BLK_DEV)[:, None] + jnp.zeros((1, NB), jnp.int32)
    offset = (safe_blocks // BLK_DEV - run_index) % cycle_size
    offset = jnp.where(offset > HOPS, offset - cycle_size, offset)
    window_index = ((offset + HOPS) * BLK_DEV + safe_blocks % BLK_DEV).astype(jnp.int32)
    window = jnp.zeros((cycle_size, window_count, BS, HEADS, HDIM), jnp.float32)
    window = window.at[run_index, window_index].add(slot_terms)
    window = to_half(window)
    positions = jnp.arange(window_count, dtype=jnp.int32)
    target = (jnp.arange(cycle_size, dtype=jnp.int32)[:, None] + positions[None, :] // BLK_DEV - HOPS) % cycle_size * BLK_DEV + positions[None, :] % BLK_DEV
    zero_blocks = jnp.zeros((block_count, BS, HEADS, HDIM), jnp.float32)
    return zero_blocks.at[target.astype(jnp.int32)].add(window)

def one_sequence(weight, inputs):
    queries, keys, values, out_grad, slot_blocks = inputs
    block_count = SEQ // BS
    score_scale = HDIM ** (-0.5)
    slot_live = slot_blocks >= 0
    safe_blocks = jnp.where(slot_live, slot_blocks, 0).astype(jnp.int32)
    query_heads = queries.reshape(block_count, BS, HEADS, HDIM).astype(jnp.float32)
    key_blocks = keys.reshape(block_count, BS, HEADS, HDIM).astype(jnp.float32)
    value_blocks = values.reshape(block_count, BS, HEADS, HDIM).astype(jnp.float32)
    key_sel = key_blocks[safe_blocks]
    value_sel = value_blocks[safe_blocks]
    scores = jnp.einsum('bqhd,bnkhd->bhqnk', query_heads, key_sel) * score_scale
    scores = jnp.where(slot_live[:, None, None, :, None], scores, -jnp.inf)
    row_max = lax.optimization_barrier(jnp.max(scores, axis=(3, 4), keepdims=True))
    row_sum = lax.optimization_barrier(jnp.sum(jnp.exp(scores - row_max), axis=(3, 4), keepdims=True))
    log_total = row_max + jnp.log(row_sum)
    probs_full = jnp.exp(scores - log_total)
    probs_half = to_half(probs_full)
    attended = to_half(jnp.einsum('bhqnk,bnkhd->bqhd', probs_half, value_sel))
    attended_flat = attended.reshape(SEQ, HW).astype(jnp.bfloat16)
    outputs = jnp.dot(attended_flat, weight.T, preferred_element_type=jnp.float32).astype(jnp.bfloat16)
    rows_grad = jnp.dot(out_grad, weight, preferred_element_type=jnp.float32)
    grad_heads = to_half(rows_grad).reshape(block_count, BS, HEADS, HDIM)
    row_delta = jnp.einsum('bqhd,bqhd->bhq', grad_heads, attended)
    prob_grad = jnp.einsum('bqhd,bnkhd->bhqnk', grad_heads, value_sel)
    dscore = to_half(probs_full * (prob_grad - row_delta[..., None, None]) * score_scale)
    query_grad = jnp.einsum('bhqnk,bnkhd->bqhd', dscore, key_sel)
    slot_mask = slot_live[:, :, None, None, None]
    key_slot = jnp.where(slot_mask, jnp.einsum('bhqnk,bqhd->bnkhd', dscore, query_heads), 0.0)
    value_slot = jnp.where(slot_mask, jnp.einsum('bhqnk,bqhd->bnkhd', probs_half, grad_heads), 0.0)
    key_grad = run_sum(key_slot, safe_blocks, block_count)
    value_grad = run_sum(value_slot, safe_blocks, block_count)
    seg_count = SEQ // TOK_DEV

    def add_partial(running, pair_rows):
        grad_cols, attn_cols = pair_rows
        return (running + to_half(jnp.dot(grad_cols.T, attn_cols, preferred_element_type=jnp.float32)), None)
    partial_sum, _ = lax.scan(add_partial, jnp.zeros((D, HW), jnp.float32), (out_grad.reshape(seg_count, TOK_DEV, D), attended_flat.reshape(seg_count, TOK_DEV, HW)))
    return (outputs, query_grad.reshape(SEQ, HW).astype(jnp.bfloat16), key_grad.reshape(SEQ, HW).astype(jnp.bfloat16), value_grad.reshape(SEQ, HW).astype(jnp.bfloat16), partial_sum)

def reference(queries, keys, values, out_grad, weight, neighbours):

    def per_sequence(running, inputs):
        results = one_sequence(weight, inputs)
        return (running + results[4], (results[0], results[1], results[2], results[3]))
    weight_sum, stacked = lax.scan(per_sequence, jnp.zeros((D, HW), jnp.float32), (queries, keys, values, out_grad, neighbours))
    weight_grad = weight_sum * (1.0 / math.sqrt(SEQS * SEQ))
    return (stacked[0], stacked[1], stacked[2], stacked[3], weight_grad)
```

```python
import math

import jax
import jax.numpy as jnp
from jax import lax
from jax.experimental import pallas as pl
from jax.experimental.pallas import tpu as pltpu
from jax.sharding import PartitionSpec as P

MESH = pl.DeviceIdType.MESH
F32 = jnp.float32
BF16 = jnp.bfloat16

HEADS = 8
HDIM = 128
BS = 128
HW = 1024
D = 2048
CHUNKS = 2
CW = HW // CHUNKS
CHEADS = HEADS // CHUNKS
NF = 16
NC = 32
NZ = 8
NY = 4
SCALE = HDIM**-0.5
DEAD = -1e30
HALF = BS // 2
K, V, Q, G = range(4)
OWN = 4
OFFSETS = (-1, -2, 1, 2, 0)
RING = 2 * 2 * 4 * CHUNKS


def dot_nn(a, b):
    return lax.dot_general(a, b, (((1,), (0,)), ((), ())), preferred_element_type=F32)


def dot_nt(a, b):
    return lax.dot_general(a, b, (((1,), (1,)), ((), ())), preferred_element_type=F32)


def dot_tn(a, b):
    return lax.dot_general(a, b, (((0,), (0,)), ((), ())), preferred_element_type=F32)


def kernel(
    nb_ref, q_ref, k_ref, v_ref, og_ref, w_ref,
    out_ref, qg_ref, kg_ref, vg_ref, wg_ref,
    win, relay_buf, wall, att, attall, ogall, probs, stat, statw, ar1, ar2, ar3, arsrc, arsum,
    ring_s, ring_r, relay_s, relay_r, ag_s, ag_r, a2a_s, a2a_r, st_s, st_r,
    ar1_s, ar1_r, ar2_s, ar2_r, ar3_s, ar3_r,
):
    f = lax.axis_index("fsdp")
    c = lax.axis_index("ctx")
    y, x, core = f // 8, (f // 2) % 4, f % 2
    yh, z = c // NZ, c % NZ

    def fs(yy, xx, kk):
        return yy * 8 + xx * 2 + kk

    xp, xm, x2 = (x + 1) % 4, (x + 3) % 4, (x + 2) % 4
    sib = (fs(y, x, 1 - core), c)
    ynb = (fs(1 - y, x, core), c)
    right = (fs(y, xp, core), c)
    left = (fs(y, xm, core), c)
    cnext = ((c + 1) % NC, (c + NC - 1) % NC)

    def copy(src, dst, ss, rs, dev):
        return pltpu.make_async_remote_copy(
            src_ref=src, dst_ref=dst, send_sem=ss, recv_sem=rs, device_id=dev, device_id_type=MESH
        )

    barrier = pltpu.get_barrier_semaphore()

    def greet(dev):
        pl.semaphore_signal(barrier, inc=1, device_id=dev, device_id_type=MESH)

    for d in range(1, NF):
        greet(((f + d) % NF, c))
    for d in range(1, NZ):
        greet((f, yh * NZ + (z + d) % NZ))
    for d in range(1, NY):
        greet((f, (yh + d) % NY * NZ + z))
    for d in (1, 2, NC - 2, NC - 1):
        greet((f, (c + d) % NC))
    pl.semaphore_wait(barrier, NF - 1 + NZ - 1 + NY - 1 + 4)

    source = {K: k_ref, V: v_ref, Q: q_ref}

    def cols(chunk):
        return pl.ds(chunk * CW, CW)

    def ring_index(item, chunk, way, hop):
        return ((item * CHUNKS + chunk) * 2 + way) * 2 + hop

    def ring_dst(item, chunk, way, hop):
        return win.at[item, 2 * way + hop, :, cols(chunk)]

    def ring_src(item, chunk, way, hop):
        if hop == 1:
            return win.at[item, 2 * way, :, cols(chunk)]
        if item == G:
            return win.at[item, OWN, :, cols(chunk)]
        return source[item].at[:, cols(chunk)]

    wrap_z = (NZ - 1, 0)

    def ring_send(item, chunk, hop):
        for way in range(2):
            i = ring_index(item, chunk, way, hop)
            src, dst = ring_src(item, chunk, way, hop), ring_dst(item, chunk, way, hop)
            dev = (f, cnext[way])

            @pl.when(z != wrap_z[way])
            def _():
                copy(src, dst, ring_s.at[i], ring_r.at[i], dev).start()

            @pl.when(z == wrap_z[way])
            def _():
                lo, hi = pl.ds(0, HALF), pl.ds(HALF, HALF)
                copy(src.at[lo], dst.at[lo], ring_s.at[i], ring_r.at[i], dev).start()
                copy(
                    src.at[hi], relay_buf.at[i], ring_s.at[i], relay_r.at[i], (f, yh * NZ + (NZ - 1 - z))
                ).start()

    def relay_copy(item, chunk, way, hop):
        i = ring_index(item, chunk, way, hop)
        dst = ring_dst(item, chunk, way, hop).at[pl.ds(HALF, HALF)]
        to = (f, (yh + (1 if way == 0 else NY - 1)) % NY * NZ + z)
        return copy(relay_buf.at[i], dst, relay_s.at[i], ring_r.at[i], to)

    def relay(item, chunk, hop):
        for way in range(2):
            i = ring_index(item, chunk, way, hop)

            @pl.when(z == wrap_z[1 - way])
            def _():
                copy(relay_buf.at[i], relay_buf.at[i], relay_s.at[i], relay_r.at[i], sib).wait_recv()
                relay_copy(item, chunk, way, hop).start()

    def ring_wait(item, chunk, hop):
        for way in range(2):
            i = ring_index(item, chunk, way, hop)
            dst = ring_dst(item, chunk, way, hop)
            copy(dst, dst, ring_s.at[i], ring_r.at[i], sib).wait_recv()

    def ring_step(items, hop, forward):
        for item, chunk in items:
            relay(item, chunk, hop)
        for item, chunk in items:
            ring_wait(item, chunk, hop)
            if forward:
                ring_send(item, chunk, hop + 1)

    lo, hi, full = pl.ds(0, HALF), pl.ds(HALF, HALF), pl.ds(0, BS)

    class Gather:
        def __init__(self, number, src, dst, width):
            self.n, self.src, self.dst, self.width = number, src, dst, width

        def block(self, yy, xx, kk, part=full):
            row = pl.multiple_of(fs(yy, xx, kk) * BS, BS) + part.start
            return self.dst.at[pl.ds(pl.multiple_of(row, HALF), part.size), self.width]

        def send(self, i, src, dst, dev):
            copy(src, dst, ag_s.at[self.n, i], ag_r.at[self.n, i], dev).start()

        def got(self, i, ref):
            copy(ref, ref, ag_s.at[self.n, i], ag_r.at[self.n, i], sib).wait_recv()

        def sent(self):
            sizes = {5: HALF, 6: HALF, 7: HALF, 8: HALF}
            for i in range(17):
                ref = self.block(0, 0, 0, pl.ds(0, sizes.get(i, BS)))
                copy(ref, ref, ag_s.at[self.n, i], ag_r.at[self.n, i], sib).wait_send()

        def first(self):
            mine = self.block(y, x, core)
            self.send(0, self.src, mine, ynb)
            self.send(1, self.src, mine, right)
            self.send(2, self.src, mine, left)
            self.send(9, self.src, mine, sib)

        def second(self):
            ref = self.block(1 - y, x, core)
            self.got(0, ref)
            self.send(3, ref, ref, right)
            self.send(4, ref, ref, left)
            self.send(10, ref, ref, sib)

        def third(self, far):
            yy = 1 - y if far else y
            a, b = (3, 4) if far else (1, 2)
            ha, hb = (7, 8) if far else (5, 6)
            sa, sb = (13, 14) if far else (11, 12)
            ref = self.block(yy, xm, core)
            self.got(a, ref)
            part = self.block(yy, xm, core, lo)
            self.send(ha, part, part, right)
            self.send(sa, ref, ref, sib)
            ref = self.block(yy, xp, core)
            self.got(b, ref)
            part = self.block(yy, xp, core, hi)
            self.send(hb, part, part, left)
            self.send(sb, ref, ref, sib)

        def fourth(self, far):
            yy = 1 - y if far else y
            ha, hb = (7, 8) if far else (5, 6)
            s = 16 if far else 15
            self.got(ha, self.block(yy, x2, core, lo))
            self.got(hb, self.block(yy, x2, core, hi))
            ref = self.block(yy, x2, core)
            self.send(s, ref, ref, sib)

        def last(self):
            for i in range(9, 17):
                self.got(i, self.block(0, 0, 0))

    gather_w = Gather(0, w_ref, wall, pl.ds(0, HW))
    gather_a = [Gather(1 + ch, att.at[:, cols(ch)], attall, cols(ch)) for ch in range(CHUNKS)]

    def own_att(ch):
        mine = pl.ds(pl.multiple_of(f * BS, BS), BS)
        attall[mine, cols(ch)] = att[:, cols(ch)]

    lane_block = lax.broadcasted_iota(jnp.int32, (1, 5 * BS), 1) // BS

    def mask_row(row_of, name_of):
        row = jnp.zeros((1, 5 * BS), F32)
        for s, off in enumerate(OFFSETS):
            r, name = row_of(off), name_of(off)
            live = nb_ref[r, 0] == name
            for n in range(1, 4):
                live = live | (nb_ref[r, n] == name)
            row = jnp.where(lane_block == s, jnp.where(live, 0.0, DEAD), row)
        return row

    lane = lax.broadcasted_iota(jnp.int32, (BS, BS), 1)

    def head_cols(h):
        return pl.ds(pl.multiple_of(h * HDIM, HDIM), HDIM)

    def window(item, h):
        return win[item, :, :, head_cols(h)].reshape(5 * BS, HDIM)

    def forward(ch, bias):
        def one(h, acc):
            s = dot_nt(q_ref[:, head_cols(h)], window(K, h)) * SCALE + bias
            m = jnp.max(s, axis=1, keepdims=True)
            e = jnp.exp(s - m)
            total = jnp.sum(e, axis=1, keepdims=True)
            p = e * (1.0 / total)
            probs[h] = p
            att[:, head_cols(h)] = dot_nn(p.astype(BF16), window(V, h)).astype(BF16)
            return jnp.where(lane == h, m + jnp.log(total), acc)

        stat[...] = lax.fori_loop(ch * CHEADS, (ch + 1) * CHEADS, one, stat[...])

    def backward_queries():
        def one(h, acc):
            g = win[G, OWN, :, head_cols(h)]
            delta = jnp.sum(
                g.astype(F32) * att[:, head_cols(h)].astype(F32), axis=1, keepdims=True
            )
            dp = dot_nt(g, window(V, h))
            ds = (probs[h] * (dp - delta) * SCALE).astype(BF16)
            qg_ref[:, head_cols(h)] = dot_nn(ds, window(K, h)).astype(BF16)
            return jnp.where(lane == h + HEADS, delta, acc)

        stat[...] = lax.fori_loop(0, HEADS, one, stat[...])

    def backward_keys(ch, bias):
        def one(h, _):
            row = lambda r: jnp.concatenate(
                [statw[s, pl.ds(r, 1), :] for s in range(5)], axis=1
            )
            q, g = window(Q, h), window(G, h)
            st = dot_nt(k_ref[:, head_cols(h)], q) * SCALE + bias
            pt = jnp.exp(st - row(h))
            dpt = dot_nt(v_ref[:, head_cols(h)], g)
            dst = (pt * (dpt - row(h + HEADS)) * SCALE).astype(BF16)
            vg_ref[:, head_cols(h)] = dot_nn(pt.astype(BF16), g).astype(BF16)
            kg_ref[:, head_cols(h)] = dot_nn(dst, q).astype(BF16)
            return 0

        lax.fori_loop(ch * CHEADS, (ch + 1) * CHEADS, one, 0)

    def zdev(d):
        return (f, yh * NZ + (z + d) % NZ)

    def ydev(d):
        return (f, (yh + d) % NY * NZ + z)

    AR = BS // NZ
    my_rows = pl.ds(pl.multiple_of(z * AR, AR), AR)

    def ar1_copy(ch, d):
        rows = pl.ds(pl.multiple_of((z + d) % NZ * AR, AR), AR)
        return copy(
            arsrc.at[ch, rows], ar1.at[ch, d - 1], ar1_s.at[ch, d - 1], ar1_r.at[ch, d - 1], zdev(d)
        )

    def ar2_copy(ch, d):
        return copy(
            ar2.at[ch, yh], ar2.at[ch, yh], ar2_s.at[ch, d - 1], ar2_r.at[ch, d - 1], ydev(d)
        )

    def ar3_copy(ch, d):
        return copy(
            ar3.at[ch, my_rows], ar3.at[ch, my_rows], ar3_s.at[ch, d - 1], ar3_r.at[ch, d - 1], zdev(d)
        )

    def reduce_first(ch):
        part = dot_tn(ogall[...], attall[:, cols(ch)])
        arsum[ch] = part
        arsrc[ch] = part.astype(BF16)
        for d in range(1, NZ):
            ar1_copy(ch, d).start()

    def reduce_second(ch):
        total = arsum[ch, my_rows]
        for d in range(1, NZ):
            ar1_copy(ch, d).wait_recv()
            total = total + ar1[ch, d - 1].astype(F32)
        ar2[ch, yh] = total.astype(BF16)
        for d in range(1, NY):
            ar2_copy(ch, d).start()

    def reduce_third(ch):
        for d in range(1, NY):
            ar2_copy(ch, d).wait_recv()
        total = ar2[ch, 0].astype(F32)
        for i in range(1, NY):
            total = total + ar2[ch, i].astype(F32)
        ar3[ch, my_rows] = (total * (1.0 / math.sqrt(NF * NC * BS))).astype(BF16)
        for d in range(1, NZ):
            ar3_copy(ch, d).start()

    def reduce_last(ch):
        for d in range(1, NZ):
            ar3_copy(ch, d).wait_recv()
        wg_ref[:, cols(ch)] = ar3[ch].astype(F32)

    def a2a_copy(d):
        to = (f + d) % NF
        return copy(
            og_ref.at[:, pl.ds(pl.multiple_of(to * BS, BS), BS)],
            ogall.at[pl.ds(pl.multiple_of(f * BS, BS), BS)],
            a2a_s.at[d - 1], a2a_r.at[d - 1], (to, c),
        )

    def stat_copy(s):
        return copy(
            statw.at[OWN], statw.at[s], st_s.at[s], st_r.at[s], (f, (c - OFFSETS[s] + NC) % NC)
        )

    for item, ch in ((K, 0), (V, 0), (K, 1), (V, 1)):
        ring_send(item, ch, 0)
    gather_w.first()
    wall[pl.ds(pl.multiple_of(f * BS, BS), BS), :] = w_ref[...]
    for item in (K, V, Q):
        win[item, OWN] = source[item][...]
    ogall[pl.ds(pl.multiple_of(f * BS, BS), BS), :] = og_ref[:, pl.ds(pl.multiple_of(f * BS, BS), BS)]
    stat[...] = jnp.zeros((BS, BS), F32)
    bias_q = mask_row(lambda off: c, lambda off: (c + off + NC) % NC)
    bias_k = mask_row(lambda off: (c + off + NC) % NC, lambda off: c)

    ring_step([(K, 0), (V, 0)], 0, True)
    gather_w.second()
    gather_w.third(False)
    ring_step([(K, 1), (V, 1)], 0, True)
    for ch in range(CHUNKS):
        ring_send(Q, ch, 0)
    gather_w.third(True)
    ring_step([(K, 0), (V, 0)], 1, False)
    forward(0, bias_q)
    gather_a[0].first()
    own_att(0)
    gather_w.fourth(False)
    gather_w.fourth(True)
    gather_w.last()
    for ch in range(CHUNKS):
        win[G, OWN, :, cols(ch)] = dot_nn(og_ref[...], wall[:, cols(ch)]).astype(BF16)
    for d in range(1, NF):
        a2a_copy(d).start()
    gather_a[0].second()
    ring_step([(K, 1), (V, 1)], 1, False)
    forward(1, bias_q)
    gather_a[1].first()
    own_att(1)
    ring_step([(Q, 0), (Q, 1)], 0, True)
    for ch in range(CHUNKS):
        ring_send(G, ch, 0)
    gather_a[0].third(False)
    backward_queries()
    statw[OWN] = stat[...].T[0 : 2 * HEADS]
    for s in range(4):
        stat_copy(s).start()
    gather_a[0].third(True)
    gather_a[1].second()
    gather_a[1].third(False)
    gather_a[0].fourth(False)
    gather_a[0].fourth(True)
    gather_a[0].last()
    for d in range(1, NF):
        a2a_copy(d).wait_recv()
    reduce_first(0)
    ring_step([(Q, 0), (Q, 1)], 1, False)
    gather_a[1].third(True)
    ring_step([(G, 0), (G, 1)], 0, True)
    gather_a[1].fourth(False)
    gather_a[1].fourth(True)
    gather_a[1].last()
    reduce_first(1)
    reduce_second(0)
    for i in range(4):
        rows = pl.ds(i * (D // 4), D // 4)
        out_ref[:, rows] = dot_nt(att[...], wall[rows, :]).astype(BF16)
    reduce_third(0)
    reduce_second(1)
    for s in range(4):
        stat_copy(s).wait_recv()
    ring_step([(G, 0)], 1, False)
    backward_keys(0, bias_k)
    reduce_third(1)
    ring_step([(G, 1)], 1, False)
    backward_keys(1, bias_k)
    for ch in range(CHUNKS):
        reduce_last(ch)

    for item in (K, V, Q, G):
        for ch in range(CHUNKS):
            for hop in range(2):
                for way in range(2):
                    i = ring_index(item, ch, way, hop)
                    dst = ring_dst(item, ch, way, hop)
                    copy(dst, dst, ring_s.at[i], ring_r.at[i], sib).wait_send()

                    @pl.when(z == wrap_z[1 - way])
                    def _():
                        relay_copy(item, ch, way, hop).wait_send()

    gather_w.sent()
    for ch in range(CHUNKS):
        gather_a[ch].sent()
        for d in range(1, NZ):
            ar1_copy(ch, d).wait_send()
            ar3_copy(ch, d).wait_send()
        for d in range(1, NY):
            ar2_copy(ch, d).wait_send()
    for d in range(1, NF):
        a2a_copy(d).wait_send()
    for s in range(4):
        stat_copy(s).wait_send()


def body(queries, keys, values, out_grad, weight, neighbours):
    vmem = pl.BlockSpec(memory_space=pltpu.VMEM)
    dma = pltpu.SemaphoreType.DMA
    outs = pl.pallas_call(
        kernel,
        name="layer",
        out_shape=(
            jax.ShapeDtypeStruct((BS, D), BF16),
            jax.ShapeDtypeStruct((BS, HW), BF16),
            jax.ShapeDtypeStruct((BS, HW), BF16),
            jax.ShapeDtypeStruct((BS, HW), BF16),
            jax.ShapeDtypeStruct((BS, HW), F32),
        ),
        in_specs=[pl.BlockSpec(memory_space=pltpu.SMEM)] + [vmem] * 5,
        out_specs=[vmem] * 5,
        scratch_shapes=[
            pltpu.VMEM((4, 5, BS, HW), BF16),
            pltpu.VMEM((RING, HALF, CW), BF16),
            pltpu.VMEM((D, HW), BF16),
            pltpu.VMEM((BS, HW), BF16),
            pltpu.VMEM((NF * BS, HW), BF16),
            pltpu.VMEM((NF * BS, BS), BF16),
            pltpu.VMEM((HEADS, BS, 5 * BS), F32),
            pltpu.VMEM((BS, BS), F32),
            pltpu.VMEM((5, 2 * HEADS, BS), F32),
            pltpu.VMEM((CHUNKS, NZ - 1, BS // NZ, CW), BF16),
            pltpu.VMEM((CHUNKS, NY, BS // NZ, CW), BF16),
            pltpu.VMEM((CHUNKS, BS, CW), BF16),
            pltpu.VMEM((CHUNKS, BS, CW), BF16),
            pltpu.VMEM((CHUNKS, BS, CW), F32),
            dma((RING,)), dma((RING,)), dma((RING,)), dma((RING,)),
            dma((1 + CHUNKS, 17)), dma((1 + CHUNKS, 17)),
            dma((NF - 1,)), dma((NF - 1,)),
            dma((4,)), dma((4,)),
            dma((CHUNKS, NZ - 1)), dma((CHUNKS, NZ - 1)),
            dma((CHUNKS, NY - 1)), dma((CHUNKS, NY - 1)),
            dma((CHUNKS, NZ - 1)), dma((CHUNKS, NZ - 1)),
        ],
        compiler_params=pltpu.CompilerParams(
            collective_id=0, has_side_effects=True, vmem_limit_bytes=48 * 2**20
        ),
        cost_estimate=pl.CostEstimate(
            flops=3 * 10**9, bytes_accessed=8 * 2**20, transcendentals=2 * 10**6
        ),
    )(neighbours[0], queries[0], keys[0], values[0], out_grad[0], weight)
    return (outs[0][None], outs[1][None], outs[2][None], outs[3][None], outs[4])


def solution(mesh):
    rows = P("fsdp", "ctx", None)
    return jax.shard_map(
        body,
        mesh=mesh,
        in_specs=(rows, rows, rows, rows, P("fsdp", None), P("fsdp", None, None)),
        out_specs=(rows, rows, rows, rows, P("fsdp", None)),
        check_vma=False,
    )
```

```python
import math

import jax
import jax.numpy as jnp
from jax import lax
from jax.experimental import pallas as pl
from jax.experimental.pallas import tpu as pltpu
from jax.sharding import PartitionSpec as P

MESH = pl.DeviceIdType.MESH
F32 = jnp.float32
BF16 = jnp.bfloat16

HEADS = 8
HDIM = 128
BS = 128
HW = 1024
D = 2048
CHUNKS = 2
CW = HW // CHUNKS
CHEADS = HEADS // CHUNKS
NF = 16
NC = 32
NZ = 8
NY = 4
SCALE = HDIM**-0.5
DEAD = -1e30
HALF = BS // 2
K, V, Q, G = range(4)
OWN = 4
OFFSETS = (-1, -2, 1, 2, 0)
RING = 2 * 2 * 4 * CHUNKS


def dot_nn(a, b):
    return lax.dot_general(a, b, (((1,), (0,)), ((), ())), preferred_element_type=F32)


def dot_nt(a, b):
    return lax.dot_general(a, b, (((1,), (1,)), ((), ())), preferred_element_type=F32)


def dot_tn(a, b):
    return lax.dot_general(a, b, (((0,), (0,)), ((), ())), preferred_element_type=F32)


def kernel(
    nb_in, q_in, k_in, v_in, og_in, w_in,
    out_hbm, qg_hbm, kg_hbm, vg_hbm, wg_hbm,
    nb_ref, out_ref, qg_ref, kg_ref, vg_ref, wg_ref,
    win, relay_buf, og, wall, att, attall, ogall, probs, stat, statw, ar1, ar2, ar3, arsrc, ar2src, arsum,
    in_s, out_s, ring_s, ring_r, relay_s, relay_r, ag_s, ag_r, a2a_s, a2a_r, st_s, st_r,
    ar1_s, ar1_r, ar2_s, ar2_r, ar3_s, ar3_r,
):
    f = lax.axis_index("fsdp")
    c = lax.axis_index("ctx")
    y, x, core = f // 8, (f // 2) % 4, f % 2
    yh, z = c // NZ, c % NZ

    def fs(yy, xx, kk):
        return yy * 8 + xx * 2 + kk

    xp, xm, x2 = (x + 1) % 4, (x + 3) % 4, (x + 2) % 4
    sib = (fs(y, x, 1 - core), c)
    ynb = (fs(1 - y, x, core), c)
    right = (fs(y, xp, core), c)
    left = (fs(y, xm, core), c)
    ycross = (fs(1 - y, x, core), (yh + jnp.where(y == 1, 1, NY - 1)) % NY * NZ + z)

    def copy(src, dst, ss, rs, dev):
        return pltpu.make_async_remote_copy(
            src_ref=src, dst_ref=dst, send_sem=ss, recv_sem=rs, device_id=dev, device_id_type=MESH
        )

    my_w = pl.ds(pl.multiple_of(f * BS, BS), BS)
    arguments = [
        pltpu.make_async_copy(src, dst, in_s.at[i])
        for i, (src, dst) in enumerate(
            (
                (k_in, win.at[K, OWN]),
                (v_in, win.at[V, OWN]),
                (w_in, wall.at[my_w]),
                (q_in, win.at[Q, OWN]),
                (og_in, og),
                (nb_in, nb_ref),
            )
        )
    ]
    for argument in arguments:
        argument.start()

    barrier = pltpu.get_barrier_semaphore()

    def greet(dev):
        pl.semaphore_signal(barrier, inc=1, device_id=dev, device_id_type=MESH)

    mine8 = x * 2 + core
    ymine = yh * 2 + y

    def xdev(d):
        return (y * 8 + (mine8 + d) % 8, c)

    def ydev(d):
        to = (ymine + d) % 8
        return (fs(to % 2, x, core), to // 2 * NZ + z)

    def zdev(d):
        return (f, yh * NZ + (z + d) % NZ)

    for d in range(1, 8):
        greet(xdev(d))
        greet(ydev(d))
        greet(zdev(d))
    for d in (1, 2, NC - 2, NC - 1):
        greet((f, (c + d) % NC))
    pl.semaphore_wait(barrier, 3 * 7 + 4)

    def cols(chunk):
        return pl.ds(chunk * CW, CW)

    def ring_index(item, chunk, way, hop):
        return ((item * CHUNKS + chunk) * 2 + way) * 2 + hop

    def ring_dst(item, chunk, way, hop):
        return win.at[item, 2 * way + hop, :, cols(chunk)]

    def ring_src(item, chunk, way, hop):
        if hop == 1:
            return win.at[item, 2 * way, :, cols(chunk)]
        return win.at[item, OWN, :, cols(chunk)]

    wrap_z = (NZ - 1, 0)

    near = jnp.where(z == 0, 1, 0)
    NEAR, FAR = near, 1 - near

    def ring_send(item, chunk, way, hop):
        i = ring_index(item, chunk, way, hop)
        src, dst = ring_src(item, chunk, way, hop), ring_dst(item, chunk, way, hop)
        dev = (f, (c + NC + 1 - 2 * way) % NC)
        leaves = z == (NZ - 1) * (1 - way)

        @pl.when(jnp.logical_not(leaves))
        def _():
            copy(src, dst, ring_s.at[0], ring_r.at[i], dev).start()

        @pl.when(leaves)
        def _():
            lo, hi = pl.ds(0, HALF), pl.ds(HALF, HALF)
            j = relay_index(item, chunk, hop)
            copy(src.at[hi], relay_buf.at[j], ring_s.at[0], relay_r.at[j], (f, yh * NZ + (NZ - 1 - z))).start()
            copy(src.at[lo], dst.at[lo], ring_s.at[0], ring_r.at[i], dev).start()

    def relay_index(item, chunk, hop):
        return (item * CHUNKS + chunk) * 2 + hop

    def relay_copy(item, chunk, way, hop):
        i, j = ring_index(item, chunk, way, hop), relay_index(item, chunk, hop)
        dst = ring_dst(item, chunk, way, hop).at[pl.ds(HALF, HALF)]
        to = (f, (yh + (1 if way == 0 else NY - 1)) % NY * NZ + z)
        return copy(relay_buf.at[j], dst, relay_s.at[0], ring_r.at[i], to)

    def relay(item, chunk, hop):
        for way in range(2):
            j = relay_index(item, chunk, hop)

            @pl.when(z == wrap_z[1 - way])
            def _():
                copy(relay_buf.at[j], relay_buf.at[j], relay_s.at[0], relay_r.at[j], sib).wait_recv()
                relay_copy(item, chunk, way, hop).start()

    def ring_wait(item, chunk, way, hop):
        i = ring_index(item, chunk, way, hop)
        dst = ring_dst(item, chunk, way, hop)
        copy(dst, dst, ring_s.at[0], ring_r.at[i], sib).wait_recv()

    def relays(items, hop):
        for item, chunk in items:
            relay(item, chunk, hop)

    def ring_take(items, hop, ways, forward):
        for item, chunk in items:
            for way in ways:
                ring_wait(item, chunk, way, hop)
                if forward:
                    ring_send(item, chunk, way, hop + 1)

    lo, hi, full = pl.ds(0, HALF), pl.ds(HALF, HALF), pl.ds(0, BS)

    class Gather:
        def __init__(self, number, src, dst, width, one_y):
            self.n, self.src, self.dst, self.width = number, src, dst, width
            self.one_y = one_y

        def block(self, yy, xx, kk, part=full):
            yy = 0 if self.one_y else yy
            row = pl.multiple_of(fs(yy, xx, kk) * BS, BS) + part.start
            return self.dst.at[pl.ds(pl.multiple_of(row, HALF), part.size), self.width]

        def send(self, i, src, dst, dev):
            copy(src, dst, ag_s.at[self.n], ag_r.at[self.n, i], dev).start()

        def got(self, i, ref):
            copy(ref, ref, ag_s.at[self.n], ag_r.at[self.n, i], sib).wait_recv()

        def first(self):
            mine = self.block(y, x, core)
            if not self.one_y:
                self.send(0, self.src.at[lo], self.block(y, x, core, lo), ynb)
                self.send(0, self.src.at[hi], self.block(y, x, core, hi), ycross)
            self.send(1, self.src, mine, right)
            self.send(2, self.src, mine, left)
            self.send(7, self.src, mine, sib)

        def second(self):
            ref = self.block(1 - y, x, core)
            self.got(0, ref)
            self.send(3, ref, ref, right)
            self.send(4, ref, ref, left)
            self.send(7, ref, ref, sib)

        def third(self, far):
            yy = 1 - y if far else y
            a, b = (3, 4) if far else (1, 2)
            h = 6 if far else 5
            ref = self.block(yy, xm, core)
            self.got(a, ref)
            part = self.block(yy, xm, core, lo)
            self.send(h, part, part, right)
            self.send(7, ref, ref, sib)
            ref = self.block(yy, xp, core)
            self.got(b, ref)
            part = self.block(yy, xp, core, hi)
            self.send(h, part, part, left)
            self.send(7, ref, ref, sib)

        def fourth(self, far):
            ref = self.block(1 - y if far else y, x2, core)
            self.got(6 if far else 5, ref)
            self.send(7, ref, ref, sib)

        def last(self):
            self.got(7, self.dst.at[pl.ds(0, (4 if self.one_y else 8) * BS), self.width])

    gather_w = Gather(0, wall.at[my_w], wall, pl.ds(0, HW), False)
    gather_a = [
        Gather(1 + ch, att.at[:, cols(ch)], attall, cols(ch), True) for ch in range(CHUNKS)
    ]
    my_tokens = pl.ds(pl.multiple_of(mine8 * BS, BS), BS)

    def own_att(ch):
        attall[my_tokens, cols(ch)] = att[:, cols(ch)]

    lane_block = lax.broadcasted_iota(jnp.int32, (1, 5 * BS), 1) // BS

    def mask_row(row_of, name_of):
        row = jnp.zeros((1, 5 * BS), F32)
        for s, off in enumerate(OFFSETS):
            r, name = row_of(off), name_of(off)
            live = nb_ref[0, r] == name
            for n in range(1, 4):
                live = live | (nb_ref[n, r] == name)
            row = jnp.where(lane_block == s, jnp.where(live, 0.0, DEAD), row)
        return row

    lane = lax.broadcasted_iota(jnp.int32, (BS, BS), 1)

    def head_cols(h):
        return pl.ds(pl.multiple_of(h * HDIM, HDIM), HDIM)

    def window(item, h):
        return win[item, :, :, head_cols(h)].reshape(5 * BS, HDIM)

    def forward(ch, bias):
        def one(h, acc):
            s = dot_nt(win[Q, OWN, :, head_cols(h)], window(K, h)) * SCALE + bias
            m = jnp.max(s, axis=1, keepdims=True)
            e = jnp.exp(s - m)
            total = jnp.sum(e, axis=1, keepdims=True)
            p = e * (1.0 / total)
            probs[h] = p
            att[:, head_cols(h)] = dot_nn(p.astype(BF16), window(V, h)).astype(BF16)
            return jnp.where(lane == h, m + jnp.log(total), acc)

        stat[...] = lax.fori_loop(ch * CHEADS, (ch + 1) * CHEADS, one, stat[...])

    def backward_queries():
        def one(h, acc):
            g = win[G, OWN, :, head_cols(h)]
            delta = jnp.sum(
                g.astype(F32) * att[:, head_cols(h)].astype(F32), axis=1, keepdims=True
            )
            dp = dot_nt(g, window(V, h))
            ds = (probs[h] * (dp - delta) * SCALE).astype(BF16)
            qg_ref[:, head_cols(h)] = dot_nn(ds, window(K, h)).astype(BF16)
            return jnp.where(lane == h + HEADS, delta, acc)

        stat[...] = lax.fori_loop(0, HEADS, one, stat[...])

    def backward_keys(ch, bias):
        def one(h, _):
            row = lambda r: jnp.concatenate(
                [statw[s, pl.ds(r, 1), :] for s in range(5)], axis=1
            )
            q, g = window(Q, h), window(G, h)
            st = dot_nt(win[K, OWN, :, head_cols(h)], q) * SCALE + bias
            pt = jnp.exp(st - row(h))
            dpt = dot_nt(win[V, OWN, :, head_cols(h)], g)
            dst = (pt * (dpt - row(h + HEADS)) * SCALE).astype(BF16)
            vg_ref[:, head_cols(h)] = dot_nn(pt.astype(BF16), g).astype(BF16)
            kg_ref[:, head_cols(h)] = dot_nn(dst, q).astype(BF16)
            return 0

        lax.fori_loop(ch * CHEADS, (ch + 1) * CHEADS, one, 0)

    AR = BS // NZ
    my_rows = pl.ds(pl.multiple_of(z * AR, AR), AR)

    def ar1_copy(ch, d):
        rows = pl.ds(pl.multiple_of((z + d) % NZ * AR, AR), AR)
        return copy(
            arsrc.at[ch, :, rows], ar1.at[ch, d - 1], ar1_s.at[ch], ar1_r.at[ch], zdev(d)
        )

    def ar2_copy(ch, d):
        return copy(
            ar2src.at[ch, (ymine + d) % 2], ar2.at[ch, ymine], ar2_s.at[ch], ar2_r.at[ch], ydev(d)
        )

    def ar3_copy(ch, d):
        return copy(
            ar3.at[ch, my_rows], ar3.at[ch, my_rows], ar3_s.at[ch], ar3_r.at[ch], zdev(d)
        )

    def arrived(ref, sem):
        copy(ref, ref, sem, sem, sib).wait_recv()

    def reduce_first(ch):
        part = dot_tn(ogall[...], attall[:, cols(ch)]).reshape(2, BS, CW)
        arsum[ch] = part
        arsrc[ch] = part.astype(BF16)
        for d in range(1, NZ):
            ar1_copy(ch, d).start()

    def reduce_second(ch):
        total = arsum[ch, :, my_rows]
        arrived(ar1.at[ch], ar1_r.at[ch])
        for d in range(1, NZ):
            total = total + ar1[ch, d - 1].astype(F32)
        ar2src[ch] = total.astype(BF16)
        ar2[ch, ymine] = ar2src[ch, y]
        for d in range(1, 8):
            ar2_copy(ch, d).start()

    def reduce_third(ch):
        arrived(ar2.at[ch, 0:7], ar2_r.at[ch])
        total = ar2[ch, 0].astype(F32)
        for i in range(1, 8):
            total = total + ar2[ch, i].astype(F32)
        ar3[ch, my_rows] = (total * (1.0 / math.sqrt(NF * NC * BS))).astype(BF16)
        for d in range(1, NZ):
            ar3_copy(ch, d).start()

    def reduce_last(ch):
        arrived(ar3.at[ch, pl.ds(0, 7 * AR)], ar3_r.at[ch])
        wg_ref[:, cols(ch)] = ar3[ch].astype(F32)

    def a2a_copy(d, yl):
        to = (mine8 + d) % 8
        return copy(
            og.at[:, pl.ds(pl.multiple_of((yl * 8 + to) * BS, BS), BS)],
            ogall.at[my_tokens, pl.ds(yl * BS, BS)],
            a2a_s.at[0], a2a_r.at[0], xdev(d),
        )

    results = [
        (out_ref, out_hbm), (qg_ref, qg_hbm), (kg_ref, kg_hbm), (vg_ref, vg_hbm), (wg_ref, wg_hbm)
    ]

    def result_copy(i, ch):
        src, dst = results[i]
        half = src.shape[1] // CHUNKS
        part = pl.ds(ch * half, half)
        return pltpu.make_async_copy(src.at[:, part], dst.at[:, part], out_s.at[i, ch])

    def stat_copy(s):
        return copy(
            statw.at[OWN], statw.at[s], st_s.at[0], st_r.at[0], (f, (c - OFFSETS[s] + NC) % NC)
        )

    KV0, KV1 = [(K, 0), (V, 0)], [(K, 1), (V, 1)]
    QS, GS = [(Q, 0), (Q, 1)], [(G, 0), (G, 1)]
    BOTH = (NEAR, FAR)
    arguments[0].wait()
    arguments[1].wait()
    for item, ch in KV0:
        for way in BOTH:
            ring_send(item, ch, way, 0)
    arguments[2].wait()
    gather_w.first()
    for item, ch in KV1:
        for way in BOTH:
            ring_send(item, ch, way, 0)
    arguments[3].wait()
    arguments[4].wait()
    for d in range(1, 8):
        for yl in range(2):
            a2a_copy(d, yl).start()
    arguments[5].wait()
    for yl in range(2):
        ogall[my_tokens, pl.ds(yl * BS, BS)] = og[:, pl.ds(pl.multiple_of((yl * 8 + mine8) * BS, BS), BS)]
    stat[...] = jnp.zeros((BS, BS), F32)
    bias_q = mask_row(lambda off: c, lambda off: (c + off + NC) % NC)
    bias_k = mask_row(lambda off: (c + off + NC) % NC, lambda off: c)

    relays(KV0, 0)
    ring_take(KV0, 0, (NEAR,), True)
    gather_w.third(False)
    relays(KV1, 0)
    ring_take(KV1, 0, (NEAR,), True)
    ring_take(KV0, 0, (FAR,), True)
    gather_w.second()
    relays(KV0, 1)
    ring_take(KV1, 0, (FAR,), True)
    for item, ch in QS:
        for way in BOTH:
            ring_send(item, ch, way, 0)
    gather_w.third(True)
    relays(KV1, 1)
    ring_take(KV0, 1, BOTH, False)
    forward(0, bias_q)
    gather_a[0].first()
    own_att(0)
    relays(QS, 0)
    ring_take(QS, 0, (NEAR,), True)
    gather_w.fourth(False)
    gather_w.fourth(True)
    ring_take(KV1, 1, BOTH, False)
    forward(1, bias_q)
    gather_a[1].first()
    own_att(1)
    gather_a[0].third(False)
    gather_w.last()
    for ch in range(CHUNKS):
        win[G, OWN, :, cols(ch)] = dot_nn(og[...], wall[:, cols(ch)]).astype(BF16)
    for item, ch in GS:
        for way in BOTH:
            ring_send(item, ch, way, 0)
    ring_take(QS, 0, (FAR,), True)
    gather_a[0].fourth(False)
    relays(QS, 1)
    gather_a[1].third(False)
    backward_queries()
    statw[OWN] = stat[...].T[0 : 2 * HEADS]
    for s in range(4):
        stat_copy(s).start()
    result_copy(1, 0).start()
    result_copy(1, 1).start()
    gather_a[0].last()
    arrived(ogall.at[pl.ds(0, 7 * BS)], a2a_r.at[0])
    reduce_first(0)
    ring_take(GS, 0, (NEAR,), True)
    gather_a[1].fourth(False)
    relays(GS, 0)
    gather_a[1].last()
    reduce_first(1)
    for i in range(4):
        rows = pl.ds(i * (D // 4), D // 4)
        out_ref[:, rows] = dot_nt(att[...], wall[rows, :]).astype(BF16)
    result_copy(0, 0).start()
    result_copy(0, 1).start()
    ring_take(GS, 0, (FAR,), True)
    reduce_second(0)
    relays(GS, 1)
    reduce_second(1)
    ring_take(QS, 1, BOTH, False)
    arrived(statw.at[0:4], st_r.at[0])
    reduce_third(0)
    reduce_third(1)
    ring_take(GS[:1], 1, BOTH, False)
    backward_keys(0, bias_k)
    result_copy(2, 0).start()
    result_copy(3, 0).start()
    ring_take(GS[1:], 1, BOTH, False)
    backward_keys(1, bias_k)
    result_copy(2, 1).start()
    result_copy(3, 1).start()
    for ch in range(CHUNKS):
        reduce_last(ch)
        result_copy(4, ch).start()

    def all_sent(ref, sem):
        copy(ref, ref, sem, sem, sib).wait_send()

    all_sent(win.at[:, 0:4], ring_s.at[0])

    @pl.when((z == 0) | (z == NZ - 1))
    def _():
        all_sent(relay_buf, relay_s.at[0])

    all_sent(wall.at[pl.ds(0, 15 * BS)], ag_s.at[0])
    for ch in range(CHUNKS):
        all_sent(attall.at[pl.ds(0, 7 * BS), cols(ch)], ag_s.at[1 + ch])
        all_sent(ar1.at[ch], ar1_s.at[ch])
        all_sent(ar2.at[ch, 0:7], ar2_s.at[ch])
        all_sent(ar3.at[ch, pl.ds(0, 7 * AR)], ar3_s.at[ch])
    all_sent(ogall.at[pl.ds(0, 7 * BS)], a2a_s.at[0])
    all_sent(statw.at[0:4], st_s.at[0])
    for i in range(5):
        for ch in range(CHUNKS):
            result_copy(i, ch).wait()


def hand_over(*refs):
    ins, outs, held, in_s, out_s = refs[:5], refs[5:10], refs[10:15], refs[15], refs[16]
    come = [pltpu.make_async_copy(ins[i], held[i], in_s.at[i]) for i in range(5)]
    go = [pltpu.make_async_copy(held[i], outs[i], out_s.at[i]) for i in range(5)]
    for copy in come:
        copy.start()
    for i in range(5):
        come[i].wait()
        go[i].start()
    for copy in go:
        copy.wait()


def body(queries, keys, values, out_grad, weight, neighbours):
    dma = pltpu.SemaphoreType.DMA
    outs = pl.pallas_call(
        kernel,
        name="layer",
        out_shape=(
            jax.ShapeDtypeStruct((BS, D), BF16),
            jax.ShapeDtypeStruct((BS, HW), BF16),
            jax.ShapeDtypeStruct((BS, HW), BF16),
            jax.ShapeDtypeStruct((BS, HW), BF16),
            jax.ShapeDtypeStruct((BS, HW), F32),
        ),
        in_specs=[pl.BlockSpec(memory_space=pl.ANY)] * 6,
        out_specs=[pl.BlockSpec(memory_space=pl.ANY)] * 5,
        scratch_shapes=[
            pltpu.SMEM((4, NC), jnp.int32),
            pltpu.VMEM((BS, D), BF16),
            pltpu.VMEM((BS, HW), BF16),
            pltpu.VMEM((BS, HW), BF16),
            pltpu.VMEM((BS, HW), BF16),
            pltpu.VMEM((BS, HW), F32),
            pltpu.VMEM((4, 5, BS, HW), BF16),
            pltpu.VMEM((RING // 2, HALF, CW), BF16),
            pltpu.VMEM((BS, D), BF16),
            pltpu.VMEM((D, HW), BF16),
            pltpu.VMEM((BS, HW), BF16),
            pltpu.VMEM((8 * BS, HW), BF16),
            pltpu.VMEM((8 * BS, 2 * BS), BF16),
            pltpu.VMEM((HEADS, BS, 5 * BS), F32),
            pltpu.VMEM((BS, BS), F32),
            pltpu.VMEM((5, 2 * HEADS, BS), F32),
            pltpu.VMEM((CHUNKS, NZ - 1, 2, BS // NZ, CW), BF16),
            pltpu.VMEM((CHUNKS, 8, BS // NZ, CW), BF16),
            pltpu.VMEM((CHUNKS, BS, CW), BF16),
            pltpu.VMEM((CHUNKS, 2, BS, CW), BF16),
            pltpu.VMEM((CHUNKS, 2, BS // NZ, CW), BF16),
            pltpu.VMEM((CHUNKS, 2, BS, CW), F32),
            dma((6,)), dma((5, CHUNKS)),
            dma((1,)), dma((RING,)), dma((1,)), dma((RING // 2,)),
            dma((1 + CHUNKS,)), dma((1 + CHUNKS, 8)),
            dma((1,)), dma((1,)),
            dma((1,)), dma((1,)),
            dma((CHUNKS,)), dma((CHUNKS,)),
            dma((CHUNKS,)), dma((CHUNKS,)),
            dma((CHUNKS,)), dma((CHUNKS,)),
        ],
        compiler_params=pltpu.CompilerParams(
            collective_id=0, has_side_effects=True, vmem_limit_bytes=62 * 2**20
        ),
        cost_estimate=pl.CostEstimate(
            flops=3 * 10**9, bytes_accessed=8 * 2**20, transcendentals=2 * 10**6
        ),
    )(neighbours[0].T, queries[0], keys[0], values[0], out_grad[0], weight)
    placed = pl.pallas_call(
        hand_over,
        name="hand_over",
        out_shape=tuple(jax.ShapeDtypeStruct(o.shape, o.dtype) for o in outs),
        in_specs=[pl.BlockSpec(memory_space=pl.ANY)] * 5,
        out_specs=[pl.BlockSpec(memory_space=pl.ANY)] * 5,
        scratch_shapes=[pltpu.VMEM(o.shape, o.dtype) for o in outs] + [dma((5,)), dma((5,))],
        cost_estimate=pl.CostEstimate(flops=0, bytes_accessed=4 * 2**20, transcendentals=0),
    )(*outs)
    return (placed[0][None], placed[1][None], placed[2][None], placed[3][None], placed[4])


def solution(mesh):
    rows = P("fsdp", "ctx", None)
    return jax.shard_map(
        body,
        mesh=mesh,
        in_specs=(rows, rows, rows, rows, P("fsdp", None), P("fsdp", None, None)),
        out_specs=(rows, rows, rows, rows, P("fsdp", None)),
        check_vma=False,
    )
```

```python
import math

import jax
import jax.numpy as jnp
from jax import lax
from jax.experimental import pallas as pl
from jax.experimental.pallas import tpu as pltpu
from jax.sharding import PartitionSpec as P

MESH = pl.DeviceIdType.MESH
F32 = jnp.float32
BF16 = jnp.bfloat16

HEADS = 8
HDIM = 128
BS = 128
HW = 1024
D = 2048
CHUNKS = 2
CW = HW // CHUNKS
CHEADS = HEADS // CHUNKS
NF = 16
NC = 32
NZ = 8
NY = 4
SCALE = HDIM**-0.5
DEAD = -1e30
HALF = BS // 2
K, V, Q, G = range(4)
OWN = 4
OFFSETS = (-1, -2, 1, 2, 0)
RING = 2 * 2 * 4 * CHUNKS


def dot_nn(a, b):
    return lax.dot_general(a, b, (((1,), (0,)), ((), ())), preferred_element_type=F32)


def dot_nt(a, b):
    return lax.dot_general(a, b, (((1,), (1,)), ((), ())), preferred_element_type=F32)


def dot_tn(a, b):
    return lax.dot_general(a, b, (((0,), (0,)), ((), ())), preferred_element_type=F32)


def kernel(
    nb_in, q_in, k_in, v_in, og_in, w_in,
    out_hbm, qg_hbm, kg_hbm, vg_hbm, wg_hbm,
    nb_ref, out_ref, qg_ref, kg_ref, vg_ref, wg_ref,
    win, relay_buf, og, wall, att, attall, ogall, probs, stat, statw, arother, arx, ar1, ar2, ar3, arsrc, arsum,
    in_s, out_s, ring_s, ring_r, relay_s, relay_r, ag_s, ag_r, a2a_s, a2a_r, st_s, st_r,
    ar0_s, ar0_r, ar1_s, ar1_r, ar2_s, ar2_r, ar3_s, ar3_r,
):
    f = lax.axis_index("fsdp")
    c = lax.axis_index("ctx")
    y, x, core = f // 8, (f // 2) % 4, f % 2
    yh, z = c // NZ, c % NZ

    def fs(yy, xx, kk):
        return yy * 8 + xx * 2 + kk

    xp, xm, x2 = (x + 1) % 4, (x + 3) % 4, (x + 2) % 4
    sib = (fs(y, x, 1 - core), c)
    ynb = (fs(1 - y, x, core), c)
    right = (fs(y, xp, core), c)
    left = (fs(y, xm, core), c)
    ycross = (fs(1 - y, x, core), (yh + jnp.where(y == 1, 1, NY - 1)) % NY * NZ + z)

    def copy(src, dst, ss, rs, dev):
        return pltpu.make_async_remote_copy(
            src_ref=src, dst_ref=dst, send_sem=ss, recv_sem=rs, device_id=dev, device_id_type=MESH
        )

    my_w = pl.ds(pl.multiple_of(f * BS, BS), BS)
    arguments = [
        pltpu.make_async_copy(src, dst, in_s.at[i])
        for i, (src, dst) in enumerate(
            (
                (k_in, win.at[K, OWN]),
                (v_in, win.at[V, OWN]),
                (w_in, wall.at[my_w]),
                (q_in, win.at[Q, OWN]),
                (og_in, og),
                (nb_in, nb_ref),
            )
        )
    ]
    for argument in arguments:
        argument.start()

    barrier = pltpu.get_barrier_semaphore()

    def greet(dev):
        pl.semaphore_signal(barrier, inc=1, device_id=dev, device_id_type=MESH)

    mine8 = x * 2 + core
    ymine = yh * 2 + y

    def xdev(d):
        return (y * 8 + (mine8 + d) % 8, c)

    def ydev(d):
        to = (ymine + d) % 8
        return (fs(to % 2, x, core), to // 2 * NZ + z)

    def zdev(d):
        return (f, yh * NZ + (z + d) % NZ)

    for d in range(1, 8):
        greet(xdev(d))
        greet(ydev(d))
        greet(zdev(d))
    for d in (1, 2, NC - 2, NC - 1):
        greet((f, (c + d) % NC))
    pl.semaphore_wait(barrier, 3 * 7 + 4)

    def cols(chunk):
        return pl.ds(chunk * CW, CW)

    def ring_index(item, chunk, way, hop):
        return ((item * CHUNKS + chunk) * 2 + way) * 2 + hop

    def ring_dst(item, chunk, way, hop):
        return win.at[item, 2 * way + hop, :, cols(chunk)]

    def ring_src(item, chunk, way, hop):
        if hop == 1:
            return win.at[item, 2 * way, :, cols(chunk)]
        return win.at[item, OWN, :, cols(chunk)]

    wrap_z = (NZ - 1, 0)

    near = jnp.where(z == 0, 1, 0)
    NEAR, FAR = near, 1 - near
    inner = (z != 0) & (z != NZ - 1)

    def ring_send(item, chunk, way, hop):
        i = ring_index(item, chunk, way, hop)
        src, dst = ring_src(item, chunk, way, hop), ring_dst(item, chunk, way, hop)
        dev = (f, (c + NC + 1 - 2 * way) % NC)
        leaves = z == (NZ - 1) * (1 - way)

        @pl.when(jnp.logical_not(leaves))
        def _():
            copy(src, dst, ring_s.at[0], ring_r.at[i], dev).start()

        @pl.when(leaves)
        def _():
            lo, hi = pl.ds(0, HALF), pl.ds(HALF, HALF)
            j = relay_index(item, chunk, hop)
            copy(src.at[hi], relay_buf.at[j], ring_s.at[0], relay_r.at[j], (f, yh * NZ + (NZ - 1 - z))).start()
            copy(src.at[lo], dst.at[lo], ring_s.at[0], ring_r.at[i], dev).start()

    def relay_index(item, chunk, hop):
        return (item * CHUNKS + chunk) * 2 + hop

    def relay_copy(item, chunk, way, hop):
        i, j = ring_index(item, chunk, way, hop), relay_index(item, chunk, hop)
        dst = ring_dst(item, chunk, way, hop).at[pl.ds(HALF, HALF)]
        to = (f, (yh + (1 if way == 0 else NY - 1)) % NY * NZ + z)
        return copy(relay_buf.at[j], dst, relay_s.at[0], ring_r.at[i], to)

    def relay(item, chunk, hop):
        for way in range(2):
            j = relay_index(item, chunk, hop)

            @pl.when(z == wrap_z[1 - way])
            def _():
                copy(relay_buf.at[j], relay_buf.at[j], relay_s.at[0], relay_r.at[j], sib).wait_recv()
                relay_copy(item, chunk, way, hop).start()

    def ring_wait(item, chunk, way, hop):
        i = ring_index(item, chunk, way, hop)
        dst = ring_dst(item, chunk, way, hop)
        copy(dst, dst, ring_s.at[0], ring_r.at[i], sib).wait_recv()

    def relays(items, hop):
        for item, chunk in items:
            relay(item, chunk, hop)

    def ring_take(items, hop, ways, forward):
        for item, chunk in items:
            for way in ways:
                ring_wait(item, chunk, way, hop)
                if forward:
                    ring_send(item, chunk, way, hop + 1)

    lo, hi, full = pl.ds(0, HALF), pl.ds(HALF, HALF), pl.ds(0, BS)

    class Gather:
        def __init__(self, number, src, dst, width, one_y):
            self.n, self.src, self.dst, self.width = number, src, dst, width
            self.one_y = one_y

        def block(self, yy, xx, kk, part=full):
            yy = 0 if self.one_y else yy
            row = pl.multiple_of(fs(yy, xx, kk) * BS, BS) + part.start
            return self.dst.at[pl.ds(pl.multiple_of(row, HALF), part.size), self.width]

        def send(self, i, src, dst, dev):
            copy(src, dst, ag_s.at[self.n], ag_r.at[self.n, i], dev).start()

        def got(self, i, ref):
            copy(ref, ref, ag_s.at[self.n], ag_r.at[self.n, i], sib).wait_recv()

        def first(self):
            mine = self.block(y, x, core)
            if not self.one_y:
                self.send(0, self.src.at[lo], self.block(y, x, core, lo), ynb)
                self.send(0, self.src.at[hi], self.block(y, x, core, hi), ycross)
            self.send(1, self.src, mine, right)
            self.send(2, self.src, mine, left)
            self.send(7, self.src, mine, sib)

        def second(self):
            ref = self.block(1 - y, x, core)
            self.got(0, ref)
            self.send(3, ref, ref, right)
            self.send(4, ref, ref, left)
            self.send(7, ref, ref, sib)

        def third(self, far):
            yy = 1 - y if far else y
            a, b = (3, 4) if far else (1, 2)
            h = 6 if far else 5
            ref = self.block(yy, xm, core)
            self.got(a, ref)
            part = self.block(yy, xm, core, lo)
            self.send(h, part, part, right)
            self.send(7, ref, ref, sib)
            ref = self.block(yy, xp, core)
            self.got(b, ref)
            part = self.block(yy, xp, core, hi)
            self.send(h, part, part, left)
            self.send(7, ref, ref, sib)

        def fourth(self, far):
            ref = self.block(1 - y if far else y, x2, core)
            self.got(6 if far else 5, ref)
            self.send(7, ref, ref, sib)

        def last(self):
            self.got(7, self.dst.at[pl.ds(0, (4 if self.one_y else 8) * BS), self.width])

    gather_w = Gather(0, wall.at[my_w], wall, pl.ds(0, HW), False)
    gather_a = [
        Gather(1 + ch, att.at[:, cols(ch)], attall, cols(ch), True) for ch in range(CHUNKS)
    ]
    my_tokens = pl.ds(pl.multiple_of(mine8 * BS, BS), BS)

    def own_att(ch):
        attall[my_tokens, cols(ch)] = att[:, cols(ch)]

    lane_block = lax.broadcasted_iota(jnp.int32, (1, 5 * BS), 1) // BS

    def mask_row(row_of, name_of):
        row = jnp.zeros((1, 5 * BS), F32)
        for s, off in enumerate(OFFSETS):
            r, name = row_of(off), name_of(off)
            live = nb_ref[0, r] == name
            for n in range(1, 4):
                live = live | (nb_ref[n, r] == name)
            row = jnp.where(lane_block == s, jnp.where(live, 0.0, DEAD), row)
        return row

    lane = lax.broadcasted_iota(jnp.int32, (BS, BS), 1)

    def head_cols(h):
        return pl.ds(pl.multiple_of(h * HDIM, HDIM), HDIM)

    def window(item, h):
        return win[item, :, :, head_cols(h)].reshape(5 * BS, HDIM)

    def forward(ch, bias):
        def one(h, acc):
            s = dot_nt(win[Q, OWN, :, head_cols(h)], window(K, h)) * SCALE + bias
            m = jnp.max(s, axis=1, keepdims=True)
            e = jnp.exp(s - m)
            total = jnp.sum(e, axis=1, keepdims=True)
            p = e * (1.0 / total)
            probs[h] = p
            att[:, head_cols(h)] = dot_nn(p.astype(BF16), window(V, h)).astype(BF16)
            return jnp.where(lane == h, m + jnp.log(total), acc)

        stat[...] = lax.fori_loop(ch * CHEADS, (ch + 1) * CHEADS, one, stat[...], unroll=True)

    def backward_queries():
        def one(h, acc):
            g = win[G, OWN, :, head_cols(h)]
            delta = jnp.sum(
                g.astype(F32) * att[:, head_cols(h)].astype(F32), axis=1, keepdims=True
            )
            dp = dot_nt(g, window(V, h))
            ds = (probs[h] * (dp - delta) * SCALE).astype(BF16)
            qg_ref[:, head_cols(h)] = dot_nn(ds, window(K, h)).astype(BF16)
            return jnp.where(lane == h + HEADS, delta, acc)

        stat[...] = lax.fori_loop(0, HEADS, one, stat[...], unroll=True)

    def backward_keys(ch, bias):
        def one(h, _):
            row = lambda r: jnp.concatenate(
                [statw[s, pl.ds(r, 1), :] for s in range(5)], axis=1
            )
            q, g = window(Q, h), window(G, h)
            st = dot_nt(win[K, OWN, :, head_cols(h)], q) * SCALE + bias
            pt = jnp.exp(st - row(h))
            dpt = dot_nt(win[V, OWN, :, head_cols(h)], g)
            dst = (pt * (dpt - row(h + HEADS)) * SCALE).astype(BF16)
            vg_ref[:, head_cols(h)] = dot_nn(pt.astype(BF16), g).astype(BF16)
            kg_ref[:, head_cols(h)] = dot_nn(dst, q).astype(BF16)
            return 0

        lax.fori_loop(ch * CHEADS, (ch + 1) * CHEADS, one, 0, unroll=True)

    AR = BS // NZ
    my_rows = pl.ds(pl.multiple_of(z * AR, AR), AR)

    def y_copy(ch, part, dev):
        return copy(arother.at[ch, part], arx.at[ch, part], ar0_s.at[ch], ar0_r.at[ch], dev)

    def ar1_copy(ch, d):
        rows = pl.ds(pl.multiple_of((z + d) % NZ * AR, AR), AR)
        return copy(arsrc.at[ch, rows], ar1.at[ch, d - 1], ar1_s.at[ch], ar1_r.at[ch], zdev(d))

    def ar2_copy(ch, d):
        to = (f, (yh + d) % NY * NZ + z)
        return copy(ar2.at[ch, yh], ar2.at[ch, yh], ar2_s.at[ch], ar2_r.at[ch], to)

    def ar3_copy(ch, d):
        return copy(ar3.at[ch, my_rows], ar3.at[ch, my_rows], ar3_s.at[ch], ar3_r.at[ch], zdev(d))

    def arrived(ref, sem):
        copy(ref, ref, sem, sem, sib).wait_recv()

    def feature_rows(yl):
        return pl.ds(pl.multiple_of(yl * BS, BS), BS)

    def reduce_start(ch):
        arother[ch] = dot_tn(ogall[:, feature_rows(1 - y)], attall[:, cols(ch)]).astype(BF16)
        y_copy(ch, lo, ynb).start()
        y_copy(ch, hi, ycross).start()
        arsum[ch] = dot_tn(ogall[:, feature_rows(y)], attall[:, cols(ch)])

    def reduce_first(ch):
        arrived(arx.at[ch], ar0_r.at[ch])
        total = arsum[ch] + arx[ch].astype(F32)
        arsum[ch] = total
        arsrc[ch] = total.astype(BF16)
        for d in range(1, NZ):
            ar1_copy(ch, d).start()

    def reduce_second(ch):
        total = arsum[ch, my_rows]
        arrived(ar1.at[ch], ar1_r.at[ch])
        for d in range(1, NZ):
            total = total + ar1[ch, d - 1].astype(F32)
        ar2[ch, yh] = total.astype(BF16)
        for d in range(1, NY):
            ar2_copy(ch, d).start()

    def reduce_third(ch):
        arrived(ar2.at[ch, 0 : NY - 1], ar2_r.at[ch])
        total = ar2[ch, 0].astype(F32)
        for i in range(1, NY):
            total = total + ar2[ch, i].astype(F32)
        ar3[ch, my_rows] = (total * (1.0 / math.sqrt(NF * NC * BS))).astype(BF16)
        for d in range(1, NZ):
            ar3_copy(ch, d).start()

    def reduce_last(ch):
        arrived(ar3.at[ch, pl.ds(0, (NZ - 1) * AR)], ar3_r.at[ch])
        wg_ref[:, cols(ch)] = ar3[ch].astype(F32)

    def a2a_copy(d, yl):
        to = (mine8 + d) % 8
        return copy(
            og.at[:, pl.ds(pl.multiple_of((yl * 8 + to) * BS, BS), BS)],
            ogall.at[my_tokens, pl.ds(yl * BS, BS)],
            a2a_s.at[0], a2a_r.at[0], xdev(d),
        )

    results = [
        (out_ref, out_hbm), (qg_ref, qg_hbm), (kg_ref, kg_hbm), (vg_ref, vg_hbm), (wg_ref, wg_hbm)
    ]

    def result_copy(i, ch):
        src, dst = results[i]
        half = src.shape[1] // CHUNKS
        part = pl.ds(ch * half, half)
        return pltpu.make_async_copy(src.at[:, part], dst.at[:, part], out_s.at[i, ch])

    def stat_copy(s):
        return copy(
            statw.at[OWN], statw.at[s], st_s.at[0], st_r.at[0], (f, (c - OFFSETS[s] + NC) % NC)
        )

    KV0, KV1 = [(K, 0), (V, 0)], [(K, 1), (V, 1)]
    QS, GS = [(Q, 0), (Q, 1)], [(G, 0), (G, 1)]
    BOTH = (NEAR, FAR)
    arguments[0].wait()
    arguments[1].wait()
    for item, ch in KV0:
        for way in BOTH:
            ring_send(item, ch, way, 0)
    arguments[2].wait()
    gather_w.first()
    for item, ch in KV1:
        for way in BOTH:
            ring_send(item, ch, way, 0)
    arguments[3].wait()
    arguments[4].wait()
    for d in range(1, 8):
        for yl in range(2):
            a2a_copy(d, yl).start()
    arguments[5].wait()
    for yl in range(2):
        ogall[my_tokens, pl.ds(yl * BS, BS)] = og[:, pl.ds(pl.multiple_of((yl * 8 + mine8) * BS, BS), BS)]
    stat[...] = jnp.zeros((BS, BS), F32)
    bias_q = mask_row(lambda off: c, lambda off: (c + off + NC) % NC)
    bias_k = mask_row(lambda off: (c + off + NC) % NC, lambda off: c)

    relays(KV0, 0)
    ring_take(KV0, 0, (NEAR,), True)
    gather_w.third(False)
    relays(KV1, 0)
    ring_take(KV1, 0, (NEAR,), True)
    ring_take(KV0, 0, (FAR,), True)
    gather_w.second()
    relays(KV0, 1)
    ring_take(KV1, 0, (FAR,), True)
    for item, ch in QS:
        for way in BOTH:
            ring_send(item, ch, way, 0)
    gather_w.third(True)
    relays(KV1, 1)
    ring_take(KV0, 1, BOTH, False)
    forward(0, bias_q)
    gather_a[0].first()
    own_att(0)
    relays(QS, 0)
    ring_take(QS, 0, (NEAR,), True)
    gather_w.fourth(False)
    gather_w.fourth(True)
    ring_take(KV1, 1, BOTH, False)
    forward(1, bias_q)
    gather_a[1].first()
    own_att(1)
    gather_a[0].third(False)
    gather_w.last()
    for ch in range(CHUNKS):
        win[G, OWN, :, cols(ch)] = dot_nn(og[...], wall[:, cols(ch)]).astype(BF16)
    for item, ch in GS:
        for way in BOTH:
            ring_send(item, ch, way, 0)
    ring_take(QS, 0, (FAR,), True)
    gather_a[0].fourth(False)
    relays(QS, 1)
    gather_a[1].third(False)
    backward_queries()
    statw[OWN] = stat[...].T[0 : 2 * HEADS]
    for s in range(4):
        stat_copy(s).start()
    result_copy(1, 0).start()
    result_copy(1, 1).start()
    gather_a[0].last()
    arrived(ogall.at[pl.ds(0, 7 * BS)], a2a_r.at[0])
    reduce_start(0)

    @pl.when(inner)
    def _():
        ring_take(GS, 0, (NEAR,), True)

    gather_a[1].fourth(False)
    gather_a[1].last()
    reduce_start(1)

    relays(GS, 0)
    reduce_first(0)

    @pl.when(jnp.logical_not(inner))
    def _():
        ring_take(GS, 0, (NEAR,), True)

    for i in range(4):
        rows = pl.ds(i * (D // 4), D // 4)
        out_ref[:, rows] = dot_nt(att[...], wall[rows, :]).astype(BF16)
    result_copy(0, 0).start()
    result_copy(0, 1).start()
    reduce_first(1)

    ring_take(GS, 0, (FAR,), True)
    reduce_second(0)
    reduce_second(1)
    ring_take(QS, 1, BOTH, False)
    arrived(statw.at[0:4], st_r.at[0])
    reduce_third(0)
    relays(GS, 1)
    reduce_third(1)
    ring_take(GS[:1], 1, BOTH, False)
    backward_keys(0, bias_k)
    result_copy(2, 0).start()
    result_copy(3, 0).start()
    ring_take(GS[1:], 1, BOTH, False)
    backward_keys(1, bias_k)
    result_copy(2, 1).start()
    result_copy(3, 1).start()
    for ch in range(CHUNKS):
        reduce_last(ch)
        result_copy(4, ch).start()

    def all_sent(ref, sem):
        copy(ref, ref, sem, sem, sib).wait_send()

    all_sent(win.at[:, 0:4], ring_s.at[0])

    @pl.when((z == 0) | (z == NZ - 1))
    def _():
        all_sent(relay_buf, relay_s.at[0])

    all_sent(wall.at[pl.ds(0, 15 * BS)], ag_s.at[0])
    for ch in range(CHUNKS):
        all_sent(attall.at[pl.ds(0, 7 * BS), cols(ch)], ag_s.at[1 + ch])
        all_sent(ar1.at[ch], ar1_s.at[ch])
        all_sent(ar2.at[ch, 0 : NY - 1], ar2_s.at[ch])
        all_sent(arx.at[ch], ar0_s.at[ch])
        all_sent(ar3.at[ch, pl.ds(0, 7 * AR)], ar3_s.at[ch])
    all_sent(ogall.at[pl.ds(0, 7 * BS)], a2a_s.at[0])
    all_sent(statw.at[0:4], st_s.at[0])
    for i in range(5):
        for ch in range(CHUNKS):
            result_copy(i, ch).wait()


def hand_over(*refs):
    ins, outs, held, in_s, out_s = refs[:5], refs[5:10], refs[10:15], refs[15], refs[16]
    come = [pltpu.make_async_copy(ins[i], held[i], in_s.at[i]) for i in range(5)]
    go = [pltpu.make_async_copy(held[i], outs[i], out_s.at[i]) for i in range(5)]
    for copy in come:
        copy.start()
    for i in range(5):
        come[i].wait()
        go[i].start()
    for copy in go:
        copy.wait()


def body(queries, keys, values, out_grad, weight, neighbours):
    dma = pltpu.SemaphoreType.DMA
    outs = pl.pallas_call(
        kernel,
        name="layer",
        out_shape=(
            jax.ShapeDtypeStruct((BS, D), BF16),
            jax.ShapeDtypeStruct((BS, HW), BF16),
            jax.ShapeDtypeStruct((BS, HW), BF16),
            jax.ShapeDtypeStruct((BS, HW), BF16),
            jax.ShapeDtypeStruct((BS, HW), F32),
        ),
        in_specs=[pl.BlockSpec(memory_space=pl.ANY)] * 6,
        out_specs=[pl.BlockSpec(memory_space=pl.ANY)] * 5,
        scratch_shapes=[
            pltpu.SMEM((4, NC), jnp.int32),
            pltpu.VMEM((BS, D), BF16),
            pltpu.VMEM((BS, HW), BF16),
            pltpu.VMEM((BS, HW), BF16),
            pltpu.VMEM((BS, HW), BF16),
            pltpu.VMEM((BS, HW), F32),
            pltpu.VMEM((4, 5, BS, HW), BF16),
            pltpu.VMEM((RING // 2, HALF, CW), BF16),
            pltpu.VMEM((BS, D), BF16),
            pltpu.VMEM((D, HW), BF16),
            pltpu.VMEM((BS, HW), BF16),
            pltpu.VMEM((8 * BS, HW), BF16),
            pltpu.VMEM((8 * BS, 2 * BS), BF16),
            pltpu.VMEM((HEADS, BS, 5 * BS), F32),
            pltpu.VMEM((BS, BS), F32),
            pltpu.VMEM((5, 2 * HEADS, BS), F32),
            pltpu.VMEM((CHUNKS, BS, CW), BF16),
            pltpu.VMEM((CHUNKS, BS, CW), BF16),
            pltpu.VMEM((CHUNKS, NZ - 1, BS // NZ, CW), BF16),
            pltpu.VMEM((CHUNKS, NY, BS // NZ, CW), BF16),
            pltpu.VMEM((CHUNKS, BS, CW), BF16),
            pltpu.VMEM((CHUNKS, BS, CW), BF16),
            pltpu.VMEM((CHUNKS, BS, CW), F32),
            dma((6,)), dma((5, CHUNKS)),
            dma((1,)), dma((RING,)), dma((1,)), dma((RING // 2,)),
            dma((1 + CHUNKS,)), dma((1 + CHUNKS, 8)),
            dma((1,)), dma((1,)),
            dma((1,)), dma((1,)),
            dma((CHUNKS,)), dma((CHUNKS,)),
            dma((CHUNKS,)), dma((CHUNKS,)),
            dma((CHUNKS,)), dma((CHUNKS,)),
            dma((CHUNKS,)), dma((CHUNKS,)),
        ],
        compiler_params=pltpu.CompilerParams(
            collective_id=0, has_side_effects=True, vmem_limit_bytes=62 * 2**20
        ),
        cost_estimate=pl.CostEstimate(
            flops=3 * 10**9, bytes_accessed=8 * 2**20, transcendentals=2 * 10**6
        ),
    )(neighbours[0].T, queries[0], keys[0], values[0], out_grad[0], weight)
    placed = pl.pallas_call(
        hand_over,
        name="hand_over",
        out_shape=tuple(jax.ShapeDtypeStruct(o.shape, o.dtype) for o in outs),
        in_specs=[pl.BlockSpec(memory_space=pl.ANY)] * 5,
        out_specs=[pl.BlockSpec(memory_space=pl.ANY)] * 5,
        scratch_shapes=[pltpu.VMEM(o.shape, o.dtype) for o in outs] + [dma((5,)), dma((5,))],
        cost_estimate=pl.CostEstimate(flops=0, bytes_accessed=4 * 2**20, transcendentals=0),
    )(*outs)
    return (placed[0][None], placed[1][None], placed[2][None], placed[3][None], placed[4])


def solution(mesh):
    rows = P("fsdp", "ctx", None)
    return jax.shard_map(
        body,
        mesh=mesh,
        in_specs=(rows, rows, rows, rows, P("fsdp", None), P("fsdp", None, None)),
        out_specs=(rows, rows, rows, rows, P("fsdp", None)),
        check_vma=False,
    )
```

```python
import math

import jax
import jax.numpy as jnp
from jax import lax
from jax.experimental import pallas as pl
from jax.experimental.pallas import tpu as pltpu
from jax.sharding import PartitionSpec as P

MESH = pl.DeviceIdType.MESH
F32 = jnp.float32
BF16 = jnp.bfloat16

HEADS = 8
HDIM = 128
BS = 128
HW = 1024
D = 2048
CHUNKS = 2
CW = HW // CHUNKS
CHEADS = HEADS // CHUNKS
NF = 16
NC = 32
NZ = 8
NY = 4
SCALE = HDIM**-0.5
DEAD = -1e30
HALF = BS // 2
K, V, Q, G = range(4)
OWN = 4
OFFSETS = (-1, -2, 1, 2, 0)
RING = 2 * 2 * 4 * CHUNKS


def dot_nn(a, b):
    return lax.dot_general(a, b, (((1,), (0,)), ((), ())), preferred_element_type=F32)


def dot_nt(a, b):
    return lax.dot_general(a, b, (((1,), (1,)), ((), ())), preferred_element_type=F32)


def dot_tn(a, b):
    return lax.dot_general(a, b, (((0,), (0,)), ((), ())), preferred_element_type=F32)


def kernel(
    nb_in, q_in, k_in, v_in, og_in, w_in,
    out_hbm, qg_hbm, kg_hbm, vg_hbm, wg_hbm,
    nb_ref, out_ref, qg_ref, kg_ref, vg_ref, wg_ref,
    win, relay_buf, og, wall, att, attall, ogall, probs, stat, statw, arother, arx, ar1, ar2, ar3, arsrc, arsum,
    in_s, out_s, ring_s, ring_r, relay_s, relay_r, ag_s, ag_r, a2a_s, a2a_r, st_s, st_r,
    ar0_s, ar0_r, ar1_s, ar1_r, ar2_s, ar2_r, ar3_s, ar3_r,
):
    f = lax.axis_index("fsdp")
    c = lax.axis_index("ctx")
    y, x, core = f // 8, (f // 2) % 4, f % 2
    yh, z = c // NZ, c % NZ

    def fs(yy, xx, kk):
        return yy * 8 + xx * 2 + kk

    xp, xm, x2 = (x + 1) % 4, (x + 3) % 4, (x + 2) % 4
    sib = (fs(y, x, 1 - core), c)
    ynb = (fs(1 - y, x, core), c)
    right = (fs(y, xp, core), c)
    left = (fs(y, xm, core), c)
    ycross = (fs(1 - y, x, core), (yh + jnp.where(y == 1, 1, NY - 1)) % NY * NZ + z)

    def copy(src, dst, ss, rs, dev):
        return pltpu.make_async_remote_copy(
            src_ref=src, dst_ref=dst, send_sem=ss, recv_sem=rs, device_id=dev, device_id_type=MESH
        )

    my_w = pl.ds(pl.multiple_of(f * BS, BS), BS)
    arguments = [
        pltpu.make_async_copy(src, dst, in_s.at[i])
        for i, (src, dst) in enumerate(
            (
                (k_in, win.at[K, OWN]),
                (v_in, win.at[V, OWN]),
                (w_in, wall.at[my_w]),
                (q_in, win.at[Q, OWN]),
                (og_in, og),
                (nb_in, nb_ref),
            )
        )
    ]
    barrier = pltpu.get_barrier_semaphore()

    def greet(dev):
        pl.semaphore_signal(barrier, inc=1, device_id=dev, device_id_type=MESH)

    mine8 = x * 2 + core
    ymine = yh * 2 + y

    def xdev(d):
        return (y * 8 + (mine8 + d) % 8, c)

    def ydev(d):
        to = (ymine + d) % 8
        return (fs(to % 2, x, core), to // 2 * NZ + z)

    def zdev(d):
        return (f, yh * NZ + (z + d) % NZ)

    for d in range(1, 8):
        greet(xdev(d))
        greet(ydev(d))
        greet(zdev(d))
    for d in (1, 2, NC - 2, NC - 1):
        greet((f, (c + d) % NC))
    for argument in arguments:
        argument.start()
    pl.semaphore_wait(barrier, 3 * 7 + 4)

    def cols(chunk):
        return pl.ds(chunk * CW, CW)

    def ring_index(item, chunk, way, hop):
        return ((item * CHUNKS + chunk) * 2 + way) * 2 + hop

    def ring_dst(item, chunk, way, hop):
        return win.at[item, 2 * way + hop, :, cols(chunk)]

    def ring_src(item, chunk, way, hop):
        if hop == 1:
            return win.at[item, 2 * way, :, cols(chunk)]
        return win.at[item, OWN, :, cols(chunk)]

    wrap_z = (NZ - 1, 0)

    near = jnp.where(z == 0, 1, 0)
    NEAR, FAR = near, 1 - near
    inner = (z != 0) & (z != NZ - 1)

    def ring_send(item, chunk, way, hop):
        i = ring_index(item, chunk, way, hop)
        src, dst = ring_src(item, chunk, way, hop), ring_dst(item, chunk, way, hop)
        dev = (f, (c + NC + 1 - 2 * way) % NC)
        leaves = z == (NZ - 1) * (1 - way)

        @pl.when(jnp.logical_not(leaves))
        def _():
            copy(src, dst, ring_s.at[0], ring_r.at[i], dev).start()

        @pl.when(leaves)
        def _():
            if by_one_way(item, hop):
                copy(src, dst, ring_s.at[0], ring_r.at[i], dev).start()
                return
            lo, hi = pl.ds(0, HALF), pl.ds(HALF, HALF)
            j = relay_index(item, chunk, hop)
            copy(src.at[hi], relay_buf.at[j], ring_s.at[0], relay_r.at[j], (f, yh * NZ + (NZ - 1 - z))).start()
            copy(src.at[lo], dst.at[lo], ring_s.at[0], ring_r.at[i], dev).start()

    def by_one_way(item, hop):
        return item == G and hop == 1

    def relay_index(item, chunk, hop):
        return (item * CHUNKS + chunk) * 2 + hop

    def relay_copy(item, chunk, way, hop):
        i, j = ring_index(item, chunk, way, hop), relay_index(item, chunk, hop)
        dst = ring_dst(item, chunk, way, hop).at[pl.ds(HALF, HALF)]
        to = (f, (yh + (1 if way == 0 else NY - 1)) % NY * NZ + z)
        return copy(relay_buf.at[j], dst, relay_s.at[0], ring_r.at[i], to)

    def relay(item, chunk, hop):
        if by_one_way(item, hop):
            return
        for way in range(2):
            j = relay_index(item, chunk, hop)

            @pl.when(z == wrap_z[1 - way])
            def _():
                copy(relay_buf.at[j], relay_buf.at[j], relay_s.at[0], relay_r.at[j], sib).wait_recv()
                relay_copy(item, chunk, way, hop).start()

    def ring_wait(item, chunk, way, hop):
        i = ring_index(item, chunk, way, hop)
        dst = ring_dst(item, chunk, way, hop)
        copy(dst, dst, ring_s.at[0], ring_r.at[i], sib).wait_recv()

    def relays(items, hop):
        for item, chunk in items:
            relay(item, chunk, hop)

    def ring_take(items, hop, ways, forward):
        for item, chunk in items:
            for way in ways:
                ring_wait(item, chunk, way, hop)
                if forward:
                    ring_send(item, chunk, way, hop + 1)

    lo, hi, full = pl.ds(0, HALF), pl.ds(HALF, HALF), pl.ds(0, BS)

    class Gather:
        def __init__(self, number, src, dst, width, one_y):
            self.n, self.src, self.dst, self.width = number, src, dst, width
            self.one_y = one_y

        def block(self, yy, xx, kk, part=full):
            yy = 0 if self.one_y else yy
            row = pl.multiple_of(fs(yy, xx, kk) * BS, BS) + part.start
            return self.dst.at[pl.ds(pl.multiple_of(row, HALF), part.size), self.width]

        def send(self, i, src, dst, dev):
            copy(src, dst, ag_s.at[self.n], ag_r.at[self.n, i], dev).start()

        def got(self, i, ref):
            copy(ref, ref, ag_s.at[self.n], ag_r.at[self.n, i], sib).wait_recv()

        def first(self):
            mine = self.block(y, x, core)
            if not self.one_y:
                self.send(0, self.src.at[lo], self.block(y, x, core, lo), ynb)
                self.send(0, self.src.at[hi], self.block(y, x, core, hi), ycross)
            self.send(1, self.src, mine, right)
            self.send(2, self.src, mine, left)
            self.send(7, self.src, mine, sib)

        def second(self):
            ref = self.block(1 - y, x, core)
            self.got(0, ref)
            self.send(3, ref, ref, right)
            self.send(4, ref, ref, left)
            self.send(7, ref, ref, sib)

        def third(self, far):
            yy = 1 - y if far else y
            a, b = (3, 4) if far else (1, 2)
            h = 6 if far else 5
            ref = self.block(yy, xm, core)
            self.got(a, ref)
            part = self.block(yy, xm, core, lo)
            self.send(h, part, part, right)
            self.send(7, ref, ref, sib)
            ref = self.block(yy, xp, core)
            self.got(b, ref)
            part = self.block(yy, xp, core, hi)
            self.send(h, part, part, left)
            self.send(7, ref, ref, sib)

        def fourth(self, far):
            ref = self.block(1 - y if far else y, x2, core)
            self.got(6 if far else 5, ref)
            self.send(7, ref, ref, sib)

        def last(self):
            self.got(7, self.dst.at[pl.ds(0, (4 if self.one_y else 8) * BS), self.width])

    gather_w = Gather(0, wall.at[my_w], wall, pl.ds(0, HW), False)
    gather_a = [
        Gather(1 + ch, att.at[:, cols(ch)], attall, cols(ch), True) for ch in range(CHUNKS)
    ]
    my_tokens = pl.ds(pl.multiple_of(mine8 * BS, BS), BS)

    def own_att(ch):
        attall[my_tokens, cols(ch)] = att[:, cols(ch)]

    lane_block = lax.broadcasted_iota(jnp.int32, (1, 5 * BS), 1) // BS

    def mask_row(row_of, name_of):
        row = jnp.zeros((1, 5 * BS), F32)
        for s, off in enumerate(OFFSETS):
            r, name = row_of(off), name_of(off)
            live = nb_ref[0, r] == name
            for n in range(1, 4):
                live = live | (nb_ref[n, r] == name)
            row = jnp.where(lane_block == s, jnp.where(live, 0.0, DEAD), row)
        return row

    lane = lax.broadcasted_iota(jnp.int32, (BS, BS), 1)

    def head_cols(h):
        return pl.ds(pl.multiple_of(h * HDIM, HDIM), HDIM)

    def window(item, h):
        return win[item, :, :, head_cols(h)].reshape(5 * BS, HDIM)

    def forward(ch, bias):
        def one(h, acc):
            s = dot_nt(win[Q, OWN, :, head_cols(h)], window(K, h)) * SCALE + bias
            m = jnp.max(s, axis=1, keepdims=True)
            e = jnp.exp(s - m)
            total = jnp.sum(e, axis=1, keepdims=True)
            p = e * (1.0 / total)
            probs[h] = p
            att[:, head_cols(h)] = dot_nn(p.astype(BF16), window(V, h)).astype(BF16)
            return jnp.where(lane == h, m + jnp.log(total), acc)

        stat[...] = lax.fori_loop(ch * CHEADS, (ch + 1) * CHEADS, one, stat[...], unroll=True)

    def backward_queries():
        def one(h, acc):
            g = win[G, OWN, :, head_cols(h)]
            delta = jnp.sum(
                g.astype(F32) * att[:, head_cols(h)].astype(F32), axis=1, keepdims=True
            )
            dp = dot_nt(g, window(V, h))
            ds = (probs[h] * (dp - delta) * SCALE).astype(BF16)
            qg_ref[:, head_cols(h)] = dot_nn(ds, window(K, h)).astype(BF16)
            return jnp.where(lane == h + HEADS, delta, acc)

        stat[...] = lax.fori_loop(0, HEADS, one, stat[...], unroll=True)

    def backward_keys(ch, bias):
        def one(h, _):
            row = lambda r: jnp.concatenate(
                [statw[s, pl.ds(r, 1), :] for s in range(5)], axis=1
            )
            q, g = window(Q, h), window(G, h)
            st = dot_nt(win[K, OWN, :, head_cols(h)], q) * SCALE + bias
            pt = jnp.exp(st - row(h))
            dpt = dot_nt(win[V, OWN, :, head_cols(h)], g)
            dst = (pt * (dpt - row(h + HEADS)) * SCALE).astype(BF16)
            vg_ref[:, head_cols(h)] = dot_nn(pt.astype(BF16), g).astype(BF16)
            kg_ref[:, head_cols(h)] = dot_nn(dst, q).astype(BF16)
            return 0

        lax.fori_loop(ch * CHEADS, (ch + 1) * CHEADS, one, 0, unroll=True)

    AR = BS // NZ
    my_rows = pl.ds(pl.multiple_of(z * AR, AR), AR)

    def y_copy(ch, part, dev):
        return copy(arother.at[ch, part], arx.at[ch, part], ar0_s.at[ch], ar0_r.at[ch], dev)

    def ar1_copy(ch, d):
        rows = pl.ds(pl.multiple_of((z + d) % NZ * AR, AR), AR)
        return copy(arsrc.at[ch, rows], ar1.at[ch, d - 1], ar1_s.at[ch], ar1_r.at[ch], zdev(d))

    def ar2_copy(ch, d):
        to = (f, (yh + d) % NY * NZ + z)
        return copy(ar2.at[ch, yh], ar2.at[ch, yh], ar2_s.at[ch], ar2_r.at[ch], to)

    def ar3_copy(ch, d):
        return copy(ar3.at[ch, my_rows], ar3.at[ch, my_rows], ar3_s.at[ch], ar3_r.at[ch], zdev(d))

    def arrived(ref, sem):
        copy(ref, ref, sem, sem, sib).wait_recv()

    def feature_rows(yl):
        return pl.ds(pl.multiple_of(yl * BS, BS), BS)

    def reduce_start(ch):
        arother[ch] = dot_tn(ogall[:, feature_rows(1 - y)], attall[:, cols(ch)]).astype(BF16)
        y_copy(ch, lo, ynb).start()
        y_copy(ch, hi, ycross).start()
        arsum[ch] = dot_tn(ogall[:, feature_rows(y)], attall[:, cols(ch)])

    def reduce_first(ch):
        arrived(arx.at[ch], ar0_r.at[ch])
        total = arsum[ch] + arx[ch].astype(F32)
        arsum[ch] = total
        arsrc[ch] = total.astype(BF16)
        for d in range(1, NZ):
            ar1_copy(ch, d).start()

    def reduce_second(ch):
        total = arsum[ch, my_rows]
        arrived(ar1.at[ch], ar1_r.at[ch])
        for d in range(1, NZ):
            total = total + ar1[ch, d - 1].astype(F32)
        ar2[ch, yh] = total.astype(BF16)
        for d in range(1, NY):
            ar2_copy(ch, d).start()

    def reduce_third(ch):
        arrived(ar2.at[ch, 0 : NY - 1], ar2_r.at[ch])
        total = ar2[ch, 0].astype(F32)
        for i in range(1, NY):
            total = total + ar2[ch, i].astype(F32)
        ar3[ch, my_rows] = (total * (1.0 / math.sqrt(NF * NC * BS))).astype(BF16)
        for d in range(1, NZ):
            ar3_copy(ch, d).start()

    def reduce_last(ch):
        arrived(ar3.at[ch, pl.ds(0, (NZ - 1) * AR)], ar3_r.at[ch])
        wg_ref[:, cols(ch)] = ar3[ch].astype(F32)

    def a2a_copy(d, yl):
        to = (mine8 + d) % 8
        return copy(
            og.at[:, pl.ds(pl.multiple_of((yl * 8 + to) * BS, BS), BS)],
            ogall.at[my_tokens, pl.ds(yl * BS, BS)],
            a2a_s.at[0], a2a_r.at[0], xdev(d),
        )

    results = [
        (out_ref, out_hbm), (qg_ref, qg_hbm), (kg_ref, kg_hbm), (vg_ref, vg_hbm), (wg_ref, wg_hbm)
    ]

    def result_copy(i, ch):
        src, dst = results[i]
        half = src.shape[1] // CHUNKS
        part = pl.ds(ch * half, half)
        return pltpu.make_async_copy(src.at[:, part], dst.at[:, part], out_s.at[i, ch])

    def stat_copy(s):
        return copy(
            statw.at[OWN], statw.at[s], st_s.at[0], st_r.at[0], (f, (c - OFFSETS[s] + NC) % NC)
        )

    KV0, KV1 = [(K, 0), (V, 0)], [(K, 1), (V, 1)]
    QS, GS = [(Q, 0), (Q, 1)], [(G, 0), (G, 1)]
    BOTH = (NEAR, FAR)
    arguments[0].wait()
    arguments[1].wait()
    for item, ch in KV0:
        for way in BOTH:
            ring_send(item, ch, way, 0)
    arguments[2].wait()
    gather_w.first()
    for item, ch in KV1:
        for way in BOTH:
            ring_send(item, ch, way, 0)
    arguments[3].wait()
    arguments[4].wait()
    for d in range(1, 8):
        for yl in range(2):
            a2a_copy(d, yl).start()
    arguments[5].wait()
    for yl in range(2):
        ogall[my_tokens, pl.ds(yl * BS, BS)] = og[:, pl.ds(pl.multiple_of((yl * 8 + mine8) * BS, BS), BS)]
    stat[...] = jnp.zeros((BS, BS), F32)
    bias_q = mask_row(lambda off: c, lambda off: (c + off + NC) % NC)
    bias_k = mask_row(lambda off: (c + off + NC) % NC, lambda off: c)

    relays(KV0, 0)
    ring_take(KV0, 0, (NEAR,), True)
    gather_w.third(False)
    relays(KV1, 0)
    ring_take(KV1, 0, (NEAR,), True)
    ring_take(KV0, 0, (FAR,), True)
    gather_w.second()
    relays(KV0, 1)
    ring_take(KV1, 0, (FAR,), True)
    for item, ch in QS:
        for way in BOTH:
            ring_send(item, ch, way, 0)
    gather_w.third(True)
    relays(KV1, 1)
    ring_take(KV0, 1, BOTH, False)
    forward(0, bias_q)
    gather_a[0].first()
    own_att(0)
    relays(QS, 0)
    ring_take(QS, 0, (NEAR,), True)
    gather_w.fourth(False)
    gather_w.fourth(True)
    ring_take(KV1, 1, BOTH, False)
    forward(1, bias_q)
    gather_a[1].first()
    own_att(1)
    gather_a[0].third(False)
    gather_w.last()
    for ch in range(CHUNKS):
        win[G, OWN, :, cols(ch)] = dot_nn(og[...], wall[:, cols(ch)]).astype(BF16)
    for item, ch in GS:
        for way in BOTH:
            ring_send(item, ch, way, 0)
    ring_take(QS, 0, (FAR,), True)
    gather_a[0].fourth(False)
    relays(QS, 1)
    gather_a[1].third(False)
    backward_queries()
    statw[OWN] = stat[...].T[0 : 2 * HEADS]
    for s in range(4):
        stat_copy(s).start()
    result_copy(1, 0).start()
    result_copy(1, 1).start()
    gather_a[0].last()
    arrived(ogall.at[pl.ds(0, 7 * BS)], a2a_r.at[0])
    reduce_start(0)

    @pl.when(inner)
    def _():
        ring_take(GS, 0, (NEAR,), True)

    gather_a[1].fourth(False)
    gather_a[1].last()
    reduce_start(1)

    relays(GS, 0)
    reduce_first(0)

    @pl.when(jnp.logical_not(inner))
    def _():
        ring_take(GS, 0, (NEAR,), True)

    for i in range(4):
        rows = pl.ds(i * (D // 4), D // 4)
        out_ref[:, rows] = dot_nt(att[...], wall[rows, :]).astype(BF16)
    result_copy(0, 0).start()
    result_copy(0, 1).start()
    reduce_first(1)

    ring_take(GS, 0, (FAR,), True)
    reduce_second(0)
    reduce_second(1)
    ring_take(QS, 1, BOTH, False)
    arrived(statw.at[0:4], st_r.at[0])
    reduce_third(0)
    reduce_third(1)
    ring_take(GS[:1], 1, BOTH, False)
    backward_keys(0, bias_k)
    result_copy(2, 0).start()
    result_copy(3, 0).start()
    ring_take(GS[1:], 1, BOTH, False)
    backward_keys(1, bias_k)
    result_copy(2, 1).start()
    result_copy(3, 1).start()
    for ch in range(CHUNKS):
        reduce_last(ch)
        result_copy(4, ch).start()

    def all_sent(ref, sem):
        copy(ref, ref, sem, sem, sib).wait_send()

    all_sent(win.at[:, 0:4], ring_s.at[0])

    @pl.when((z == 0) | (z == NZ - 1))
    def _():
        all_sent(relay_buf.at[pl.ds(0, 14)], relay_s.at[0])

    all_sent(wall.at[pl.ds(0, 15 * BS)], ag_s.at[0])
    for ch in range(CHUNKS):
        all_sent(attall.at[pl.ds(0, 7 * BS), cols(ch)], ag_s.at[1 + ch])
        all_sent(ar1.at[ch], ar1_s.at[ch])
        all_sent(ar2.at[ch, 0 : NY - 1], ar2_s.at[ch])
        all_sent(arx.at[ch], ar0_s.at[ch])
        all_sent(ar3.at[ch, pl.ds(0, 7 * AR)], ar3_s.at[ch])
    all_sent(ogall.at[pl.ds(0, 7 * BS)], a2a_s.at[0])
    all_sent(statw.at[0:4], st_s.at[0])
    for i in range(5):
        for ch in range(CHUNKS):
            result_copy(i, ch).wait()


def hand_over(*refs):
    ins, outs, held, in_s, out_s = refs[:5], refs[5:10], refs[10:15], refs[15], refs[16]
    come = [pltpu.make_async_copy(ins[i], held[i], in_s.at[i]) for i in range(5)]
    go = [pltpu.make_async_copy(held[i], outs[i], out_s.at[i]) for i in range(5)]
    for copy in come:
        copy.start()
    for i in range(5):
        come[i].wait()
        go[i].start()
    for copy in go:
        copy.wait()


def body(queries, keys, values, out_grad, weight, neighbours):
    dma = pltpu.SemaphoreType.DMA
    outs = pl.pallas_call(
        kernel,
        name="layer",
        out_shape=(
            jax.ShapeDtypeStruct((BS, D), BF16),
            jax.ShapeDtypeStruct((BS, HW), BF16),
            jax.ShapeDtypeStruct((BS, HW), BF16),
            jax.ShapeDtypeStruct((BS, HW), BF16),
            jax.ShapeDtypeStruct((BS, HW), F32),
        ),
        in_specs=[pl.BlockSpec(memory_space=pl.ANY)] * 6,
        out_specs=[pl.BlockSpec(memory_space=pl.ANY)] * 5,
        scratch_shapes=[
            pltpu.SMEM((4, NC), jnp.int32),
            pltpu.VMEM((BS, D), BF16),
            pltpu.VMEM((BS, HW), BF16),
            pltpu.VMEM((BS, HW), BF16),
            pltpu.VMEM((BS, HW), BF16),
            pltpu.VMEM((BS, HW), F32),
            pltpu.VMEM((4, 5, BS, HW), BF16),
            pltpu.VMEM((RING // 2, HALF, CW), BF16),
            pltpu.VMEM((BS, D), BF16),
            pltpu.VMEM((D, HW), BF16),
            pltpu.VMEM((BS, HW), BF16),
            pltpu.VMEM((8 * BS, HW), BF16),
            pltpu.VMEM((8 * BS, 2 * BS), BF16),
            pltpu.VMEM((HEADS, BS, 5 * BS), F32),
            pltpu.VMEM((BS, BS), F32),
            pltpu.VMEM((5, 2 * HEADS, BS), F32),
            pltpu.VMEM((CHUNKS, BS, CW), BF16),
            pltpu.VMEM((CHUNKS, BS, CW), BF16),
            pltpu.VMEM((CHUNKS, NZ - 1, BS // NZ, CW), BF16),
            pltpu.VMEM((CHUNKS, NY, BS // NZ, CW), BF16),
            pltpu.VMEM((CHUNKS, BS, CW), BF16),
            pltpu.VMEM((CHUNKS, BS, CW), BF16),
            pltpu.VMEM((CHUNKS, BS, CW), F32),
            dma((6,)), dma((5, CHUNKS)),
            dma((1,)), dma((RING,)), dma((1,)), dma((RING // 2,)),
            dma((1 + CHUNKS,)), dma((1 + CHUNKS, 8)),
            dma((1,)), dma((1,)),
            dma((1,)), dma((1,)),
            dma((CHUNKS,)), dma((CHUNKS,)),
            dma((CHUNKS,)), dma((CHUNKS,)),
            dma((CHUNKS,)), dma((CHUNKS,)),
            dma((CHUNKS,)), dma((CHUNKS,)),
        ],
        compiler_params=pltpu.CompilerParams(
            collective_id=0, has_side_effects=True, vmem_limit_bytes=62 * 2**20
        ),
        cost_estimate=pl.CostEstimate(
            flops=3 * 10**9, bytes_accessed=8 * 2**20, transcendentals=2 * 10**6
        ),
    )(neighbours[0].T, queries[0], keys[0], values[0], out_grad[0], weight)
    placed = pl.pallas_call(
        hand_over,
        name="hand_over",
        out_shape=tuple(jax.ShapeDtypeStruct(o.shape, o.dtype) for o in outs),
        in_specs=[pl.BlockSpec(memory_space=pl.ANY)] * 5,
        out_specs=[pl.BlockSpec(memory_space=pl.ANY)] * 5,
        scratch_shapes=[pltpu.VMEM(o.shape, o.dtype) for o in outs] + [dma((5,)), dma((5,))],
        cost_estimate=pl.CostEstimate(flops=0, bytes_accessed=4 * 2**20, transcendentals=0),
    )(*outs)
    return (placed[0][None], placed[1][None], placed[2][None], placed[3][None], placed[4])


def solution(mesh):
    rows = P("fsdp", "ctx", None)
    return jax.shard_map(
        body,
        mesh=mesh,
        in_specs=(rows, rows, rows, rows, P("fsdp", None), P("fsdp", None, None)),
        out_specs=(rows, rows, rows, rows, P("fsdp", None)),
        check_vma=False,
    )
```

```python
import math

import jax
import jax.numpy as jnp
from jax import lax
from jax.experimental import pallas as pl
from jax.experimental.pallas import tpu as pltpu
from jax.sharding import PartitionSpec as P

MESH = pl.DeviceIdType.MESH
F32 = jnp.float32
BF16 = jnp.bfloat16

HEADS = 8
HDIM = 128
BS = 128
HW = 1024
D = 2048
CHUNKS = 2
CW = HW // CHUNKS
CHEADS = HEADS // CHUNKS
NF = 16
NC = 32
NZ = 8
NY = 4
SCALE = HDIM**-0.5
DEAD = -1e30
HALF = BS // 2
K, V, Q, G = range(4)
OWN = 4
OFFSETS = (-1, -2, 1, 2, 0)
RING = 2 * 2 * 4 * CHUNKS


def dot_nn(a, b):
    return lax.dot_general(a, b, (((1,), (0,)), ((), ())), preferred_element_type=F32)


def dot_nt(a, b):
    return lax.dot_general(a, b, (((1,), (1,)), ((), ())), preferred_element_type=F32)


def dot_tn(a, b):
    return lax.dot_general(a, b, (((0,), (0,)), ((), ())), preferred_element_type=F32)


def kernel(
    nb_in, q_in, k_in, v_in, og_in, w_in,
    out_hbm, qg_hbm, kg_hbm, vg_hbm, wg_hbm,
    nb_ref, out_ref, qg_ref, kg_ref, vg_ref, wg_ref,
    win, relay_buf, og, wall, att, attall, ogall, probs, stat, statw, arother, arx, ar1, ar2, ar3, arsrc, arsum,
    in_s, out_s, ring_s, ring_r, relay_s, relay_r, ag_s, ag_r, a2a_s, a2a_r, st_s, st_r,
    ar0_s, ar0_r, ar1_s, ar1_r, ar2_s, ar2_r, ar3_s, ar3_r,
):
    f = lax.axis_index("fsdp")
    c = lax.axis_index("ctx")
    y, x, core = f // 8, (f // 2) % 4, f % 2
    yh, z = c // NZ, c % NZ

    def fs(yy, xx, kk):
        return yy * 8 + xx * 2 + kk

    xp, xm, x2 = (x + 1) % 4, (x + 3) % 4, (x + 2) % 4
    sib = (fs(y, x, 1 - core), c)
    ynb = (fs(1 - y, x, core), c)
    right = (fs(y, xp, core), c)
    left = (fs(y, xm, core), c)
    ycross = (fs(1 - y, x, core), (yh + jnp.where(y == 1, 1, NY - 1)) % NY * NZ + z)

    def copy(src, dst, ss, rs, dev):
        return pltpu.make_async_remote_copy(
            src_ref=src, dst_ref=dst, send_sem=ss, recv_sem=rs, device_id=dev, device_id_type=MESH
        )

    my_w = pl.ds(pl.multiple_of(f * BS, BS), BS)
    arguments = [
        pltpu.make_async_copy(src, dst, in_s.at[i])
        for i, (src, dst) in enumerate(
            (
                (k_in, win.at[K, OWN]),
                (v_in, win.at[V, OWN]),
                (w_in, wall.at[my_w]),
                (q_in, win.at[Q, OWN]),
                (og_in, og),
                (nb_in, nb_ref),
            )
        )
    ]
    barrier = pltpu.get_barrier_semaphore()

    def greet(dev):
        pl.semaphore_signal(barrier, inc=1, device_id=dev, device_id_type=MESH)

    mine8 = x * 2 + core
    ymine = yh * 2 + y

    def xdev(d):
        return (y * 8 + (mine8 + d) % 8, c)

    def ydev(d):
        to = (ymine + d) % 8
        return (fs(to % 2, x, core), to // 2 * NZ + z)

    def zdev(d):
        return (f, yh * NZ + (z + d) % NZ)

    for d in range(1, 8):
        greet(xdev(d))
        greet(ydev(d))
        greet(zdev(d))
    for d in (1, 2, NC - 2, NC - 1):
        greet((f, (c + d) % NC))
    for argument in arguments:
        argument.start()
    pl.semaphore_wait(barrier, 3 * 7 + 4)

    def cols(chunk):
        return pl.ds(chunk * CW, CW)

    def ring_index(item, chunk, way, hop):
        return ((item * CHUNKS + chunk) * 2 + way) * 2 + hop

    def ring_dst(item, chunk, way, hop):
        return win.at[item, 2 * way + hop, :, cols(chunk)]

    def ring_src(item, chunk, way, hop):
        if hop == 1:
            return win.at[item, 2 * way, :, cols(chunk)]
        return win.at[item, OWN, :, cols(chunk)]

    wrap_z = (NZ - 1, 0)

    near = jnp.where(z == 0, 1, 0)
    NEAR, FAR = near, 1 - near
    inner = (z != 0) & (z != NZ - 1)

    def ring_send(item, chunk, way, hop):
        i = ring_index(item, chunk, way, hop)
        src, dst = ring_src(item, chunk, way, hop), ring_dst(item, chunk, way, hop)
        dev = (f, (c + NC + 1 - 2 * way) % NC)
        leaves = z == (NZ - 1) * (1 - way)

        @pl.when(jnp.logical_not(leaves))
        def _():
            copy(src, dst, ring_s.at[0], ring_r.at[i], dev).start()

        @pl.when(leaves)
        def _():
            if by_one_way(item, hop):
                copy(src, dst, ring_s.at[0], ring_r.at[i], dev).start()
                return
            lo, hi = pl.ds(0, HALF), pl.ds(HALF, HALF)
            j = relay_index(item, chunk, hop)
            copy(src.at[hi], relay_buf.at[j], ring_s.at[0], relay_r.at[j], (f, yh * NZ + (NZ - 1 - z))).start()
            copy(src.at[lo], dst.at[lo], ring_s.at[0], ring_r.at[i], dev).start()

    def by_one_way(item, hop):
        return item == G and hop == 1

    def relay_index(item, chunk, hop):
        return (item * CHUNKS + chunk) * 2 + hop

    def relay_copy(item, chunk, way, hop):
        i, j = ring_index(item, chunk, way, hop), relay_index(item, chunk, hop)
        dst = ring_dst(item, chunk, way, hop).at[pl.ds(HALF, HALF)]
        to = (f, (yh + (1 if way == 0 else NY - 1)) % NY * NZ + z)
        return copy(relay_buf.at[j], dst, relay_s.at[0], ring_r.at[i], to)

    def relay(item, chunk, hop):
        if by_one_way(item, hop):
            return
        for way in range(2):
            j = relay_index(item, chunk, hop)

            @pl.when(z == wrap_z[1 - way])
            def _():
                copy(relay_buf.at[j], relay_buf.at[j], relay_s.at[0], relay_r.at[j], sib).wait_recv()
                relay_copy(item, chunk, way, hop).start()

    def ring_wait(item, chunk, way, hop):
        i = ring_index(item, chunk, way, hop)
        dst = ring_dst(item, chunk, way, hop)
        copy(dst, dst, ring_s.at[0], ring_r.at[i], sib).wait_recv()

    def relays(items, hop):
        for item, chunk in items:
            relay(item, chunk, hop)

    def ring_take(items, hop, ways, forward):
        for item, chunk in items:
            for way in ways:
                ring_wait(item, chunk, way, hop)
                if forward:
                    ring_send(item, chunk, way, hop + 1)

    lo, hi, full = pl.ds(0, HALF), pl.ds(HALF, HALF), pl.ds(0, BS)

    class Gather:
        def __init__(self, number, src, dst, width, one_y):
            self.n, self.src, self.dst, self.width = number, src, dst, width
            self.one_y = one_y

        def block(self, yy, xx, kk, part=full):
            yy = 0 if self.one_y else yy
            row = pl.multiple_of(fs(yy, xx, kk) * BS, BS) + part.start
            return self.dst.at[pl.ds(pl.multiple_of(row, HALF), part.size), self.width]

        def send(self, i, src, dst, dev):
            copy(src, dst, ag_s.at[self.n], ag_r.at[self.n, i], dev).start()

        def got(self, i, ref):
            copy(ref, ref, ag_s.at[self.n], ag_r.at[self.n, i], sib).wait_recv()

        def first(self):
            mine = self.block(y, x, core)
            if not self.one_y:
                self.send(0, self.src.at[lo], self.block(y, x, core, lo), ynb)
                self.send(0, self.src.at[hi], self.block(y, x, core, hi), ycross)
            self.send(1, self.src, mine, right)
            self.send(2, self.src, mine, left)
            self.send(7, self.src, mine, sib)

        def second(self):
            ref = self.block(1 - y, x, core)
            self.got(0, ref)
            self.send(3, ref, ref, right)
            self.send(4, ref, ref, left)
            self.send(7, ref, ref, sib)

        def third(self, far):
            yy = 1 - y if far else y
            a, b = (3, 4) if far else (1, 2)
            h = 6 if far else 5
            ref = self.block(yy, xm, core)
            self.got(a, ref)
            part = self.block(yy, xm, core, lo)
            self.send(h, part, part, right)
            self.send(7, ref, ref, sib)
            ref = self.block(yy, xp, core)
            self.got(b, ref)
            part = self.block(yy, xp, core, hi)
            self.send(h, part, part, left)
            self.send(7, ref, ref, sib)

        def fourth(self, far):
            ref = self.block(1 - y if far else y, x2, core)
            self.got(6 if far else 5, ref)
            self.send(7, ref, ref, sib)

        def last(self):
            self.got(7, self.dst.at[pl.ds(0, (4 if self.one_y else 8) * BS), self.width])

    gather_w = Gather(0, wall.at[my_w], wall, pl.ds(0, HW), False)
    gather_a = [
        Gather(1 + ch, att.at[:, cols(ch)], attall, cols(ch), True) for ch in range(CHUNKS)
    ]
    my_tokens = pl.ds(pl.multiple_of(mine8 * BS, BS), BS)

    def own_att(ch):
        attall[my_tokens, cols(ch)] = att[:, cols(ch)]

    lane_block = lax.broadcasted_iota(jnp.int32, (1, 5 * BS), 1) // BS

    def mask_row(row_of, name_of):
        row = jnp.zeros((1, 5 * BS), F32)
        for s, off in enumerate(OFFSETS):
            r, name = row_of(off), name_of(off)
            live = nb_ref[0, r] == name
            for n in range(1, 4):
                live = live | (nb_ref[n, r] == name)
            row = jnp.where(lane_block == s, jnp.where(live, 0.0, DEAD), row)
        return row

    lane = lax.broadcasted_iota(jnp.int32, (BS, BS), 1)

    def head_cols(h):
        return pl.ds(pl.multiple_of(h * HDIM, HDIM), HDIM)

    def window(item, h):
        return win[item, :, :, head_cols(h)].reshape(5 * BS, HDIM)

    def forward(ch, bias):
        def one(h, acc):
            s = dot_nt(win[Q, OWN, :, head_cols(h)], window(K, h)) * SCALE + bias
            m = jnp.max(s, axis=1, keepdims=True)
            e = jnp.exp(s - m)
            total = jnp.sum(e, axis=1, keepdims=True)
            p = e * (1.0 / total)
            probs[h] = p
            att[:, head_cols(h)] = dot_nn(p.astype(BF16), window(V, h)).astype(BF16)
            return jnp.where(lane == h, m + jnp.log(total), acc)

        stat[...] = lax.fori_loop(ch * CHEADS, (ch + 1) * CHEADS, one, stat[...], unroll=True)

    def backward_queries():
        def one(h, acc):
            g = win[G, OWN, :, head_cols(h)]
            delta = jnp.sum(
                g.astype(F32) * att[:, head_cols(h)].astype(F32), axis=1, keepdims=True
            )
            dp = dot_nt(g, window(V, h))
            ds = (probs[h] * (dp - delta) * SCALE).astype(BF16)
            qg_ref[:, head_cols(h)] = dot_nn(ds, window(K, h)).astype(BF16)
            return jnp.where(lane == h + HEADS, delta, acc)

        stat[...] = lax.fori_loop(0, HEADS, one, stat[...], unroll=True)

    def backward_keys(ch, bias):
        def one(h, _):
            row = lambda r: jnp.concatenate(
                [statw[s, pl.ds(r, 1), :] for s in range(5)], axis=1
            )
            q, g = window(Q, h), window(G, h)
            st = dot_nt(win[K, OWN, :, head_cols(h)], q) * SCALE + bias
            pt = jnp.exp(st - row(h))
            dpt = dot_nt(win[V, OWN, :, head_cols(h)], g)
            dst = (pt * (dpt - row(h + HEADS)) * SCALE).astype(BF16)
            vg_ref[:, head_cols(h)] = dot_nn(pt.astype(BF16), g).astype(BF16)
            kg_ref[:, head_cols(h)] = dot_nn(dst, q).astype(BF16)
            return 0

        lax.fori_loop(ch * CHEADS, (ch + 1) * CHEADS, one, 0, unroll=True)

    AR = BS // NZ
    my_rows = pl.ds(pl.multiple_of(z * AR, AR), AR)

    def y_copy(ch, part, dev):
        return copy(arother.at[ch, part], arx.at[ch, part], ar0_s.at[ch], ar0_r.at[ch], dev)

    def ar1_copy(ch, d):
        rows = pl.ds(pl.multiple_of((z + d) % NZ * AR, AR), AR)
        return copy(arsrc.at[ch, rows], ar1.at[ch, d - 1], ar1_s.at[ch], ar1_r.at[ch], zdev(d))

    def ar2_copy(ch, d):
        to = (f, (yh + d) % NY * NZ + z)
        return copy(ar2.at[ch, yh], ar2.at[ch, yh], ar2_s.at[ch], ar2_r.at[ch], to)

    def ar3_copy(ch, d):
        return copy(ar3.at[ch, my_rows], ar3.at[ch, my_rows], ar3_s.at[ch], ar3_r.at[ch], zdev(d))

    def arrived(ref, sem):
        copy(ref, ref, sem, sem, sib).wait_recv()

    def feature_rows(yl):
        return pl.ds(pl.multiple_of(yl * BS, BS), BS)

    def reduce_start(ch):
        arother[ch] = dot_tn(ogall[:, feature_rows(1 - y)], attall[:, cols(ch)]).astype(BF16)
        y_copy(ch, lo, ynb).start()
        y_copy(ch, hi, ycross).start()
        arsum[ch] = dot_tn(ogall[:, feature_rows(y)], attall[:, cols(ch)])

    def reduce_first(ch):
        arrived(arx.at[ch], ar0_r.at[ch])
        total = arsum[ch] + arx[ch].astype(F32)
        arsum[ch] = total
        arsrc[ch] = total.astype(BF16)
        for d in range(1, NZ):
            ar1_copy(ch, d).start()

    def reduce_second(ch):
        total = arsum[ch, my_rows]
        arrived(ar1.at[ch], ar1_r.at[ch])
        for d in range(1, NZ):
            total = total + ar1[ch, d - 1].astype(F32)
        ar2[ch, yh] = total.astype(BF16)
        for d in range(1, NY):
            ar2_copy(ch, d).start()

    def reduce_third(ch):
        arrived(ar2.at[ch, 0 : NY - 1], ar2_r.at[ch])
        total = ar2[ch, 0].astype(F32)
        for i in range(1, NY):
            total = total + ar2[ch, i].astype(F32)
        ar3[ch, my_rows] = (total * (1.0 / math.sqrt(NF * NC * BS))).astype(BF16)
        for d in range(1, NZ):
            ar3_copy(ch, d).start()

    def reduce_last(ch):
        arrived(ar3.at[ch, pl.ds(0, (NZ - 1) * AR)], ar3_r.at[ch])
        wg_ref[:, cols(ch)] = ar3[ch].astype(F32)

    def a2a_copy(d, yl):
        to = (mine8 + d) % 8
        return copy(
            og.at[:, pl.ds(pl.multiple_of((yl * 8 + to) * BS, BS), BS)],
            ogall.at[my_tokens, pl.ds(yl * BS, BS)],
            a2a_s.at[0], a2a_r.at[0], xdev(d),
        )

    results = [
        (out_ref, out_hbm), (qg_ref, qg_hbm), (kg_ref, kg_hbm), (vg_ref, vg_hbm), (wg_ref, wg_hbm)
    ]

    def result_copy(i, ch):
        src, dst = results[i]
        half = src.shape[1] // CHUNKS
        part = pl.ds(ch * half, half)
        return pltpu.make_async_copy(src.at[:, part], dst.at[:, part], out_s.at[i, ch])

    def stat_copy(s):
        return copy(
            statw.at[OWN], statw.at[s], st_s.at[0], st_r.at[0], (f, (c - OFFSETS[s] + NC) % NC)
        )

    KV0, KV1 = [(K, 0), (V, 0)], [(K, 1), (V, 1)]
    QS, GS = [(Q, 0), (Q, 1)], [(G, 0), (G, 1)]
    BOTH = (NEAR, FAR)
    arguments[0].wait()
    arguments[1].wait()
    for item, ch in KV0:
        for way in BOTH:
            ring_send(item, ch, way, 0)
    arguments[2].wait()
    gather_w.first()
    for item, ch in KV1:
        for way in BOTH:
            ring_send(item, ch, way, 0)
    arguments[3].wait()
    arguments[4].wait()
    for d in range(1, 8):
        for yl in range(2):
            a2a_copy(d, yl).start()
    arguments[5].wait()
    for yl in range(2):
        ogall[my_tokens, pl.ds(yl * BS, BS)] = og[:, pl.ds(pl.multiple_of((yl * 8 + mine8) * BS, BS), BS)]
    stat[...] = jnp.zeros((BS, BS), F32)
    bias_q = mask_row(lambda off: c, lambda off: (c + off + NC) % NC)
    bias_k = mask_row(lambda off: (c + off + NC) % NC, lambda off: c)

    relays(KV0, 0)
    ring_take(KV0, 0, (NEAR,), True)
    gather_w.third(False)
    relays(KV1, 0)
    ring_take(KV1, 0, (NEAR,), True)
    ring_take(KV0, 0, (FAR,), True)
    gather_w.second()
    relays(KV0, 1)
    ring_take(KV1, 0, (FAR,), True)
    gather_w.third(True)
    relays(KV1, 1)
    for item, ch in QS:
        for way in BOTH:
            ring_send(item, ch, way, 0)
    ring_take(KV0, 1, BOTH, False)
    forward(0, bias_q)
    gather_a[0].first()
    own_att(0)
    relays(QS, 0)
    ring_take(QS, 0, (NEAR,), True)
    gather_w.fourth(False)
    gather_w.fourth(True)
    ring_take(KV1, 1, BOTH, False)
    forward(1, bias_q)
    gather_a[1].first()
    own_att(1)
    gather_a[0].third(False)
    gather_w.last()
    for ch in range(CHUNKS):
        win[G, OWN, :, cols(ch)] = dot_nn(og[...], wall[:, cols(ch)]).astype(BF16)
    for item, ch in GS:
        for way in BOTH:
            ring_send(item, ch, way, 0)
    ring_take(QS, 0, (FAR,), True)
    gather_a[0].fourth(False)
    relays(QS, 1)
    gather_a[1].third(False)
    backward_queries()
    statw[OWN] = stat[...].T[0 : 2 * HEADS]
    for s in range(4):
        stat_copy(s).start()
    result_copy(1, 0).start()
    result_copy(1, 1).start()
    gather_a[0].last()
    arrived(ogall.at[pl.ds(0, 7 * BS)], a2a_r.at[0])
    reduce_start(0)

    @pl.when(inner)
    def _():
        ring_take(GS, 0, (NEAR,), True)

    gather_a[1].fourth(False)
    gather_a[1].last()
    reduce_start(1)

    relays(GS, 0)
    reduce_first(0)

    @pl.when(jnp.logical_not(inner))
    def _():
        ring_take(GS, 0, (NEAR,), True)

    for i in range(4):
        rows = pl.ds(i * (D // 4), D // 4)
        out_ref[:, rows] = dot_nt(att[...], wall[rows, :]).astype(BF16)
    result_copy(0, 0).start()
    result_copy(0, 1).start()
    reduce_first(1)

    ring_take(GS, 0, (FAR,), True)
    reduce_second(0)
    reduce_second(1)
    ring_take(QS, 1, BOTH, False)
    arrived(statw.at[0:4], st_r.at[0])
    reduce_third(0)
    reduce_third(1)
    ring_take(GS[:1], 1, BOTH, False)
    backward_keys(0, bias_k)
    result_copy(2, 0).start()
    result_copy(3, 0).start()
    ring_take(GS[1:], 1, BOTH, False)
    backward_keys(1, bias_k)
    result_copy(2, 1).start()
    result_copy(3, 1).start()
    for ch in range(CHUNKS):
        reduce_last(ch)
        result_copy(4, ch).start()

    def all_sent(ref, sem):
        copy(ref, ref, sem, sem, sib).wait_send()

    all_sent(win.at[:, 0:4], ring_s.at[0])

    @pl.when((z == 0) | (z == NZ - 1))
    def _():
        all_sent(relay_buf.at[pl.ds(0, 14)], relay_s.at[0])

    all_sent(wall.at[pl.ds(0, 15 * BS)], ag_s.at[0])
    for ch in range(CHUNKS):
        all_sent(attall.at[pl.ds(0, 7 * BS), cols(ch)], ag_s.at[1 + ch])
        all_sent(ar1.at[ch], ar1_s.at[ch])
        all_sent(ar2.at[ch, 0 : NY - 1], ar2_s.at[ch])
        all_sent(arx.at[ch], ar0_s.at[ch])
        all_sent(ar3.at[ch, pl.ds(0, 7 * AR)], ar3_s.at[ch])
    all_sent(ogall.at[pl.ds(0, 7 * BS)], a2a_s.at[0])
    all_sent(statw.at[0:4], st_s.at[0])
    for i in range(5):
        for ch in range(CHUNKS):
            result_copy(i, ch).wait()


def hand_over(*refs):
    ins, outs, held, in_s, out_s = refs[:5], refs[5:10], refs[10:15], refs[15], refs[16]
    come = [pltpu.make_async_copy(ins[i], held[i], in_s.at[i]) for i in range(5)]
    go = [pltpu.make_async_copy(held[i], outs[i], out_s.at[i]) for i in range(5)]
    for copy in come:
        copy.start()
    for i in range(5):
        come[i].wait()
        go[i].start()
    for copy in go:
        copy.wait()


def body(queries, keys, values, out_grad, weight, neighbours):
    dma = pltpu.SemaphoreType.DMA
    outs = pl.pallas_call(
        kernel,
        name="layer",
        out_shape=(
            jax.ShapeDtypeStruct((BS, D), BF16),
            jax.ShapeDtypeStruct((BS, HW), BF16),
            jax.ShapeDtypeStruct((BS, HW), BF16),
            jax.ShapeDtypeStruct((BS, HW), BF16),
            jax.ShapeDtypeStruct((BS, HW), F32),
        ),
        in_specs=[pl.BlockSpec(memory_space=pl.ANY)] * 6,
        out_specs=[pl.BlockSpec(memory_space=pl.ANY)] * 5,
        scratch_shapes=[
            pltpu.SMEM((4, NC), jnp.int32),
            pltpu.VMEM((BS, D), BF16),
            pltpu.VMEM((BS, HW), BF16),
            pltpu.VMEM((BS, HW), BF16),
            pltpu.VMEM((BS, HW), BF16),
            pltpu.VMEM((BS, HW), F32),
            pltpu.VMEM((4, 5, BS, HW), BF16),
            pltpu.VMEM((RING // 2, HALF, CW), BF16),
            pltpu.VMEM((BS, D), BF16),
            pltpu.VMEM((D, HW), BF16),
            pltpu.VMEM((BS, HW), BF16),
            pltpu.VMEM((8 * BS, HW), BF16),
            pltpu.VMEM((8 * BS, 2 * BS), BF16),
            pltpu.VMEM((HEADS, BS, 5 * BS), F32),
            pltpu.VMEM((BS, BS), F32),
            pltpu.VMEM((5, 2 * HEADS, BS), F32),
            pltpu.VMEM((CHUNKS, BS, CW), BF16),
            pltpu.VMEM((CHUNKS, BS, CW), BF16),
            pltpu.VMEM((CHUNKS, NZ - 1, BS // NZ, CW), BF16),
            pltpu.VMEM((CHUNKS, NY, BS // NZ, CW), BF16),
            pltpu.VMEM((CHUNKS, BS, CW), BF16),
            pltpu.VMEM((CHUNKS, BS, CW), BF16),
            pltpu.VMEM((CHUNKS, BS, CW), F32),
            dma((6,)), dma((5, CHUNKS)),
            dma((1,)), dma((RING,)), dma((1,)), dma((RING // 2,)),
            dma((1 + CHUNKS,)), dma((1 + CHUNKS, 8)),
            dma((1,)), dma((1,)),
            dma((1,)), dma((1,)),
            dma((CHUNKS,)), dma((CHUNKS,)),
            dma((CHUNKS,)), dma((CHUNKS,)),
            dma((CHUNKS,)), dma((CHUNKS,)),
            dma((CHUNKS,)), dma((CHUNKS,)),
        ],
        compiler_params=pltpu.CompilerParams(
            collective_id=0, has_side_effects=True, vmem_limit_bytes=62 * 2**20
        ),
        cost_estimate=pl.CostEstimate(
            flops=3 * 10**9, bytes_accessed=8 * 2**20, transcendentals=2 * 10**6
        ),
    )(neighbours[0].T, queries[0], keys[0], values[0], out_grad[0], weight)
    placed = pl.pallas_call(
        hand_over,
        name="hand_over",
        out_shape=tuple(jax.ShapeDtypeStruct(o.shape, o.dtype) for o in outs),
        in_specs=[pl.BlockSpec(memory_space=pl.ANY)] * 5,
        out_specs=[pl.BlockSpec(memory_space=pl.ANY)] * 5,
        scratch_shapes=[pltpu.VMEM(o.shape, o.dtype) for o in outs] + [dma((5,)), dma((5,))],
        cost_estimate=pl.CostEstimate(flops=0, bytes_accessed=4 * 2**20, transcendentals=0),
    )(*outs)
    return (placed[0][None], placed[1][None], placed[2][None], placed[3][None], placed[4])


def solution(mesh):
    rows = P("fsdp", "ctx", None)
    return jax.shard_map(
        body,
        mesh=mesh,
        in_specs=(rows, rows, rows, rows, P("fsdp", None), P("fsdp", None, None)),
        out_specs=(rows, rows, rows, rows, P("fsdp", None)),
        check_vma=False,
    )
```
